256 devices in a mesh: seq: 32 (over x, y, core), ch: 8 (over z).
Axes of the slice: x: 4, y: 4, z: 8, core: 2. Of those that a mesh axis runs over, the one named last changes fastest.
Arguments:
- queries: bfloat16 [4096, 8192], P('seq', 'ch'), may hold values from -6 to 6
- keys: bfloat16 [4096, 8192], P('seq', 'ch'), may hold values from -6 to 6
- values: bfloat16 [4096, 8192], P('seq', 'ch'), may hold values from -6 to 6
- filters: bfloat16 [4096, 8192], P('seq', 'ch'), may hold values from -0.09375 to 0.09375
- short_weight: bfloat16 [3, 7, 8192], P(None, None, 'ch'), may hold values from -2 to 2
- skip_gain: float32 [8192], P('ch'), may hold values from -4 to 4
- residual: bfloat16 [4096, 8192], P('seq', 'ch'), may hold values from -30 to 30
- norm_gain: float32 [8192], P('ch'), may hold values from 0.5 to 1.5
Outputs:
- stream_out: bfloat16 [4096, 8192], P('seq', 'ch')
- normed: bfloat16 [4096, 8192], P('seq', 'ch')
The draws below stay inside these ranges and needn't reach their ends.
All inputs are finite; a program needn't handle non-finite values.
Results may differ from the reference program's by a relative error of at most 0.0065.
Values may be sent and summed in bfloat16 or wider, within the bound.
A program may use at most 64 MiB of HBM per device.

```python
import math
import jax
import jax.numpy as jnp
from jax import lax

D = 8192
TAPS = 7
TOKENS = 4096


def draw_residual(key, part):
    key = jax.random.fold_in(key, 5)
    key_values, key_cols, key_rows = jax.random.split(key, 3)
    column = jnp.arange(D, dtype=jnp.float32) / D
    entries = jax.random.truncated_normal(key_values, -5.0, 5.0, (TOKENS, D), jnp.float32)
    row_scale = 10.0 ** (0.3 * jax.random.uniform(key_rows, (TOKENS, 1), jnp.float32))
    column_scale = 0.3 * 10.0 ** (0.5 * column + 0.5 * jax.random.uniform(key_cols, (D,), jnp.float32))
    return (entries * row_scale * column_scale).astype(jnp.bfloat16)


def levels(key, shape, cuts, smallest, top_value):
    loudness = 1.0
    for dim, blocks in cuts:
        heights = jax.random.uniform(jax.random.fold_in(jax.random.fold_in(key, 6), dim), (blocks,), jnp.float32, smallest / len(cuts), top_value / len(cuts))
        loudness = loudness * jnp.repeat(jnp.exp(heights), shape[dim] // blocks).reshape((-1,) + (1,) * (len(shape) - 1 - dim))
    return loudness


def noise(stream_key, dims, width, reach, shards=(), kind=jnp.bfloat16):
    values = jax.random.normal(stream_key, dims, jnp.float32) * width
    if len(shards) > 0:
        values = levels(stream_key, dims, shards, -0.22, 0.18) * values
    return jnp.clip(values, min=-reach, max=reach).astype(kind)


def setup_inputs(seed: int = 0) -> dict:
    key_of = jax.random.split(jax.random.key(seed), 9)
    return {
        "queries": noise(key_of[0], (TOKENS, D), 1.0, 6.0, ((0, 32), (1, 8))),
        "keys": noise(key_of[1], (TOKENS, D), 1.0, 6.0, ((0, 32), (1, 8))),
        "values": noise(key_of[2], (TOKENS, D), 1.0, 6.0, ((0, 32), (1, 8))),
        "filters": noise(key_of[3], (TOKENS, D), TOKENS ** -0.5, 0.09375, ((0, 32), (1, 8))),
        "short_weight": noise(key_of[4], (3, TAPS, D), TAPS ** -0.5, 2.0, ((2, 8),)),
        "skip_gain": noise(key_of[5], (D,), 1.0, 4.0, ((0, 8),), jnp.float32),
        "residual": draw_residual(jax.random.fold_in(key_of[8], 71), 0),
        "norm_gain": jnp.clip(1.0 + 0.1 * jax.random.normal(key_of[7], (D,), jnp.float32), 0.5, 1.5),
    }


def short_filter(stream, weights):
    length = stream.shape[0]
    padded = jnp.pad(stream.astype(jnp.float32), ((TAPS - 1, 0), (0, 0)))
    total = jnp.zeros(stream.shape, jnp.float32)
    for offset in range(TAPS):
        start = TAPS - 1 - offset
        total = total + weights[offset].astype(jnp.float32) * padded[start:start + length]
    return total

def long_filter(mixed, filters):
    length = mixed.shape[0]
    block_width = math.gcd(D, 512)
    count = D // block_width

    def one_block(pair):
        signal, kernel = pair
        spectrum = jnp.fft.rfft(signal, n=2 * length, axis=0) * jnp.fft.rfft(kernel, n=2 * length, axis=0)
        return jnp.fft.irfft(spectrum, n=2 * length, axis=0)[:length]
    signal = mixed.astype(jnp.float32).reshape(length, count, block_width).transpose(1, 0, 2)
    kernel = filters.astype(jnp.float32).reshape(length, count, block_width).transpose(1, 0, 2)
    result = lax.map(one_block, (signal, kernel))
    return result.transpose(1, 0, 2).reshape(length, D).astype(jnp.float32)

def reference(queries, keys, values, filters, short_weight, skip_gain, residual, norm_gain):
    short_q = short_filter(queries, short_weight[0])
    short_k = short_filter(keys, short_weight[1])
    short_v = short_filter(values, short_weight[2])
    mixed = (short_k * short_v).astype(jnp.bfloat16)
    conv = long_filter(mixed, filters)
    total = residual.astype(jnp.float32) + short_q * (conv + skip_gain * mixed.astype(jnp.float32))
    stream_out = total.astype(jnp.bfloat16)
    stream_f = stream_out.astype(jnp.float32)
    power = lax.optimization_barrier(jnp.mean(stream_f * stream_f, axis=1, keepdims=True))
    normed = (stream_f * lax.rsqrt(power + 1e-05) * norm_gain).astype(jnp.bfloat16)
    return (stream_out, normed)
```

```python
import functools
import math

import jax
import jax.numpy as jnp
import numpy as np
from jax import lax
from jax.experimental import pallas as pl
from jax.experimental.pallas import tpu as pltpu
from jax.sharding import PartitionSpec as P

F32 = jnp.float32
BF16 = jnp.bfloat16
LANES = 128
GROUP = 16
PARTS = 32
ROOT = math.sqrt(0.5)

KEPT = (
    [0, 8, 16, 24, 32]
    + [1 + 8 * b for b in range(8)]
    + [2 + 8 * b for b in range(8)]
    + [3 + 8 * b for b in range(8)]
    + [4 + 8 * b for b in range(4)]
)
PLACE = {k1: i for i, k1 in enumerate(KEPT)}
ROWS = len(KEPT) * GROUP
CHUNK = 11 * GROUP


def tables():
    lane = np.arange(LANES)
    angle = 2.0 * np.pi * (np.outer(lane, lane) % LANES) / LANES
    cos, sin = np.cos(angle), np.sin(angle)
    forward = np.block([[cos, -sin], [sin, cos]])
    backward = np.block([[cos, sin], [-sin, cos]])
    parts = []
    for matrix in (forward, backward):
        high = matrix.astype(np.float32).astype(jnp.bfloat16)
        low = (matrix - high.astype(np.float64)).astype(np.float32).astype(jnp.bfloat16)
        parts += [high, low]
    matrices = np.stack(parts)
    turn = 2.0 * np.pi * np.outer(KEPT, lane) / (64 * LANES)
    weight = np.where(np.isin(KEPT, [0, 32]), 1.0, 2.0)[:, None] / (64 * LANES)
    twist = np.stack([np.cos(turn), -np.sin(turn), weight * np.cos(turn), weight * np.sin(turn)])
    return matrices, twist.astype(np.float32)


def plus(a, b):
    if a is None:
        return b
    return a if b is None else a + b


def neg(a):
    return None if a is None else -a


def minus(a, b):
    if b is None:
        return a
    return -b if a is None else a - b


def scaled(a, factor):
    return None if a is None else a * factor


def cplus(a, b):
    return (plus(a[0], b[0]), plus(a[1], b[1]))


def cminus(a, b):
    return (minus(a[0], b[0]), minus(a[1], b[1]))


def quarter(a, sign):
    return (neg(a[1]), a[0]) if sign > 0 else (a[1], neg(a[0]))


def turned(a, angle):
    cos, sin = math.cos(angle), math.sin(angle)
    if angle == 0.0:
        return a
    return (
        minus(scaled(a[0], cos), scaled(a[1], sin)),
        plus(scaled(a[1], cos), scaled(a[0], sin)),
    )


def dft4(z, sign):
    a, b = cplus(z[0], z[2]), cminus(z[0], z[2])
    c, d = cplus(z[1], z[3]), quarter(cminus(z[1], z[3]), sign)
    return [cplus(a, c), cplus(b, d), cminus(a, c), cminus(b, d)]


def dft8(z, sign):
    even, odd = dft4(z[0::2], sign), dft4(z[1::2], sign)
    a, b = odd[1], odd[3]
    if sign > 0:
        first = (scaled(minus(a[0], a[1]), ROOT), scaled(plus(a[0], a[1]), ROOT))
        third = (scaled(plus(b[0], b[1]), -ROOT), scaled(minus(b[0], b[1]), ROOT))
    else:
        first = (scaled(plus(a[0], a[1]), ROOT), scaled(minus(a[1], a[0]), ROOT))
        third = (scaled(minus(b[1], b[0]), ROOT), scaled(plus(b[0], b[1]), -ROOT))
    odd = [odd[0], first, quarter(odd[2], sign), third]
    return [cplus(e, o) for e, o in zip(even, odd)] + [cminus(e, o) for e, o in zip(even, odd)]


def forward64(x):
    column = [[None] * 8 for _ in range(5)]
    for s in range(8):
        x0, x1, x2, x3 = x[s], x[8 + s], x[16 + s], x[24 + s]
        a, b, c, d = x0 + x2, x1 + x3, x0 - x2, (x1 - x3)
        rb, rd = b * ROOT, d * ROOT
        values = [(a + b, None), (x0 + rd, -x2 - rb), (c, -d), (x0 - rd, x2 - rb), (a - b, None)]
        for k in range(5):
            column[k][s] = turned(values[k], -2.0 * math.pi * s * k / 64)
    out = {}
    for k in range(5):
        result = dft8(column[k], -1)
        for b in range((5, 8, 8, 8, 4)[k]):
            out[k + 8 * b] = result[b]
    return out


def backward64(get):
    v = []
    for k in range(5):
        count = (5, 8, 8, 8, 4)[k]
        z = [get(k + 8 * b) if b < count else (None, None) for b in range(8)]
        if k == 0:
            z[0], z[4] = (z[0][0], None), (z[4][0], None)
        u = dft8(z, 1)
        v.append([turned(u[s], 2.0 * math.pi * s * k / 64) for s in range(8)])
    y = [None] * 32
    for s in range(8):
        (a, _), (br, bi), (cr, ci), (dr, di), (e, _) = [v[k][s] for k in range(5)]
        p, m = a + e, a - e
        y[s] = (p + cr) + (br + dr)
        y[16 + s] = (p - cr) + (di - bi)
        f, g = (br - dr) * ROOT, (bi + di) * ROOT
        y[8 + s] = (m - ci) + (f - g)
        y[24 + s] = (m + ci) - (f + g)
    return y


def split(a):
    high = a.astype(BF16)
    return high, (a - high.astype(F32)).astype(BF16)


def product3(high, low, matrix_high, matrix_low):
    dot = functools.partial(jnp.dot, preferred_element_type=F32)
    return dot(high, matrix_high) + (dot(low, matrix_high) + dot(high, matrix_low))


def kernel(
    queries, keys, values, filters, short_taps, skip, residual, gain, matrices, twist,
    stream_out, normed,
    q_in, k_in, v_in, f_in, r_in, short_weight, skip_gain, norm_gain, mat, tw, halo, ext, mixed, short_q, base, stream_f, out_bf, norm_bf,
    send_f, send_m, got_f, got_m, send_y, got_y, a_high, a_low, spec_f, back, sums, own_sum,
    in_sem, halo_send, halo_recv, f_send, f_recv, m_send, m_recv, y_send, y_recv, p_send, p_recv, out_sem,
):
    parts, rounds = lax.axis_size("seq"), lax.axis_size("ch")
    me, plane = lax.axis_index("seq"), lax.axis_index("ch")
    rows, width = q_in.shape
    own = width // parts
    halves = own // GROUP
    blocks = width // LANES

    barrier = pltpu.get_barrier_semaphore()

    @pl.loop(1, parts)
    def _(d):
        pl.semaphore_signal(barrier, inc=1, device_id={"seq": lax.rem(me + d, parts)})

    @pl.loop(1, rounds)
    def _(d):
        pl.semaphore_signal(barrier, inc=1, device_id={"ch": lax.rem(plane + d, rounds)})

    loads = [
        pltpu.make_async_copy(source, target, in_sem.at[i])
        for i, (source, target) in enumerate(
            [
                (filters, f_in), (keys, k_in), (values, v_in), (queries, q_in), (residual, r_in),
                (short_taps, short_weight), (skip, skip_gain), (gain, norm_gain),
                (matrices, mat), (twist, tw),
            ]
        )
    ]
    for load in loads:
        load.start()

    def lanes(b):
        return pl.ds(pl.multiple_of(b * LANES, LANES), LANES)

    loads[0].wait()

    @pl.loop(0, blocks)
    def _(b):
        send_f[lanes(b), :] = f_in[:, lanes(b)].astype(F32).T.astype(BF16)

    for i in (1, 2, 3):
        loads[i].wait()
    for i, stream in enumerate((q_in, k_in, v_in)):
        ext[i, pl.ds(8, rows), :] = stream[...].astype(F32)

    pl.semaphore_wait(barrier, parts - 1 + rounds - 1)

    halo_copies = [
        pltpu.make_async_remote_copy(
            src_ref=stream.at[pl.ds(rows - GROUP, GROUP)],
            dst_ref=halo.at[i],
            send_sem=halo_send.at[i],
            recv_sem=halo_recv.at[i],
            device_id={"seq": lax.rem(me + 1, parts)},
        )
        for i, stream in enumerate((q_in, k_in, v_in))
    ]
    for i in (1, 2, 0):
        halo_copies[i].start()

    def own_rows(peer, h):
        return pl.ds(pl.multiple_of(peer * own + h * GROUP, GROUP), GROUP)

    def exchange(source, target, send_sem, recv_sem):
        pltpu.make_async_copy(source(me), target, recv_sem).start()

        @pl.loop(1, parts)
        def _(d):
            peer = lax.rem(me + d, parts)
            pltpu.make_async_remote_copy(
                src_ref=source(peer),
                dst_ref=target,
                send_sem=send_sem,
                recv_sem=recv_sem,
                device_id={"seq": peer},
            ).start()

    for h in range(halves):
        exchange(
            lambda peer: send_f.at[own_rows(peer, h)], got_f.at[h, me], f_send.at[h], f_recv.at[h]
        )

    for i in (1, 2):
        halo_copies[i].wait_recv()
    loads[5].wait()
    first = me == 0
    for i in (1, 2):
        ext[i, pl.ds(0, 8), :] = jnp.where(first, 0.0, halo[i].astype(F32)[8:, :])

    def short(i, b):
        weights = short_weight[i, :, lanes(b)].astype(F32)
        total = weights[0:1] * ext[i, pl.ds(8, rows), lanes(b)]
        for j in range(1, weights.shape[0]):
            total = total + weights[j : j + 1] * ext[i, pl.ds(8 - j, rows), lanes(b)]
        return total

    @pl.loop(0, blocks)
    def _(b):
        product = (short(1, b) * short(2, b)).astype(BF16)
        mixed[:, lanes(b)] = product
        send_m[lanes(b), :] = product.astype(F32).T.astype(BF16)

    for h in range(halves):
        exchange(
            lambda peer: send_m.at[own_rows(peer, h)], got_m.at[h, me], m_send.at[h], m_recv.at[h]
        )

    halo_copies[0].wait_recv()
    ext[0, pl.ds(0, 8), :] = jnp.where(first, 0.0, halo[0].astype(F32)[8:, :])
    loads[4].wait()
    loads[6].wait()

    @pl.loop(0, blocks)
    def _(b):
        gate = short(0, b)
        short_q[:, lanes(b)] = gate
        direct = skip_gain[:, lanes(b)] * mixed[:, lanes(b)].astype(F32)
        base[:, lanes(b)] = r_in[:, lanes(b)].astype(F32) + gate * direct

    loads[8].wait()
    loads[9].wait()

    def twisted(value, i, which):
        cos, sin = tw[which, pl.ds(i, 1), :], tw[which + 1, pl.ds(i, 1), :]
        if value[1] is None:
            return value[0] * cos, value[0] * sin
        return value[0] * cos - value[1] * sin, value[1] * cos + value[0] * sin

    def first_stage(got, h):
        spectrum = forward64([got[h, s].astype(F32) for s in range(PARTS)])
        for k1 in KEPT:
            i = PLACE[k1]
            for half, part in enumerate(twisted(spectrum[k1], i, 0)):
                high, low = split(part)
                place = (pl.ds(i * GROUP, GROUP), pl.ds(half * LANES, LANES))
                a_high[place] = high
                a_low[place] = low

    for h in range(halves):
        pltpu.make_async_copy(got_f.at[h], got_f.at[h], f_recv.at[h]).wait()

    @pl.loop(0, halves)
    def _(h):
        first_stage(got_f, h)
        for c in range(ROWS // CHUNK):
            chunk = pl.ds(c * CHUNK, CHUNK)
            spec_f[h, chunk, :] = product3(a_high[chunk, :], a_low[chunk, :], mat[0], mat[1])

    @pl.loop(0, halves)
    def _(h):
        pltpu.make_async_copy(got_m.at[h], got_m.at[h], m_recv.at[h]).wait()
        first_stage(got_m, h)
        for c in range(ROWS // CHUNK):
            chunk = pl.ds(c * CHUNK, CHUNK)
            signal = product3(a_high[chunk, :], a_low[chunk, :], mat[0], mat[1])
            taps = spec_f[h, chunk, :]
            sr, si = signal[:, :LANES], signal[:, LANES:]
            fr, fi = taps[:, :LANES], taps[:, LANES:]
            both = jnp.concatenate([sr * fr - si * fi, sr * fi + si * fr], axis=1)
            high, low = split(both)
            back[chunk, :] = product3(high, low, mat[2], mat[3])

        def value(k1):
            i = PLACE[k1]
            part = pl.ds(i * GROUP, GROUP)
            return twisted((back[part, pl.ds(0, LANES)], back[part, pl.ds(LANES, LANES)]), i, 2)

        for s, y in enumerate(backward64(value)):
            send_y[h, s] = y.astype(BF16)
        exchange(lambda peer: send_y.at[h, peer], got_y.at[own_rows(me, h)], y_send.at[h], y_recv)

    pltpu.make_async_copy(got_y, got_y, y_recv).wait()

    partial = jnp.zeros((rows, LANES), F32)
    for b in range(blocks):
        at = pl.ds(b * LANES, LANES)
        conv = got_y[at, :].astype(F32).T
        rounded = (base[:, at] + short_q[:, at] * conv).astype(BF16)
        out_bf[:, at] = rounded
        value = rounded.astype(F32)
        stream_f[:, at] = value
        partial = partial + value * value
    write_stream = pltpu.make_async_copy(out_bf, stream_out, out_sem.at[0])
    write_stream.start()

    own_sum[...] = jnp.broadcast_to(jnp.sum(partial.T, axis=0, keepdims=True), own_sum.shape)
    pltpu.make_async_copy(own_sum, sums.at[plane], p_recv).start()

    @pl.loop(1, rounds)
    def _(d):
        pltpu.make_async_remote_copy(
            src_ref=own_sum,
            dst_ref=sums.at[plane],
            send_sem=p_send,
            recv_sem=p_recv,
            device_id={"ch": lax.rem(plane + d, rounds)},
        ).start()

    pltpu.make_async_copy(sums, sums, p_recv).wait()
    power = jnp.sum(sums[...], axis=0)[0:1] / (width * rounds)
    loads[7].wait()
    scale = jnp.broadcast_to(lax.rsqrt(power + 1e-05), (LANES, rows)).T
    for b in range(blocks):
        at = pl.ds(b * LANES, LANES)
        norm_bf[:, at] = (stream_f[:, at] * scale * norm_gain[:, at]).astype(BF16)
    write_normed = pltpu.make_async_copy(norm_bf, normed, out_sem.at[1])
    write_normed.start()

    for copy in halo_copies:
        copy.wait_send()
    others = pl.ds(0, parts - 1)
    for h in range(halves):
        pltpu.make_async_copy(got_f.at[h, others], got_f.at[h, others], f_send.at[h]).wait()
        pltpu.make_async_copy(got_m.at[h, others], got_m.at[h, others], m_send.at[h]).wait()
        pltpu.make_async_copy(got_m.at[h, others], got_m.at[h, others], y_send.at[h]).wait()
    if rounds > 1:
        most = sums.at[pl.ds(0, rounds - 1)]
        pltpu.make_async_copy(most, most, p_send).wait()
    write_stream.wait()
    write_normed.wait()


def shards(queries, keys, values, filters, short_weight, skip_gain, residual, norm_gain):
    rows, width = queries.shape
    parts, rounds = lax.axis_size("seq"), lax.axis_size("ch")
    taps = short_weight.shape[1]
    own = width // parts
    halves = own // GROUP
    assert parts == PARTS and rows == LANES and own % GROUP == 0
    matrices, twist = tables()
    block = (rows, width)
    whole = pl.BlockSpec(memory_space=pltpu.HBM)
    dma = pltpu.SemaphoreType.DMA
    return pl.pallas_call(
        kernel,
        out_shape=(jax.ShapeDtypeStruct(block, BF16), jax.ShapeDtypeStruct(block, BF16)),
        in_specs=[whole] * 10,
        out_specs=(whole, whole),
        scratch_shapes=[
            pltpu.VMEM(block, BF16),
            pltpu.VMEM(block, BF16),
            pltpu.VMEM(block, BF16),
            pltpu.VMEM(block, BF16),
            pltpu.VMEM(block, BF16),
            pltpu.VMEM((3, taps, width), BF16),
            pltpu.VMEM((1, width), F32),
            pltpu.VMEM((1, width), F32),
            pltpu.VMEM(matrices.shape, BF16),
            pltpu.VMEM(twist.shape, F32),
            pltpu.VMEM((3, GROUP, width), BF16),
            pltpu.VMEM((3, rows + 8, width), F32),
            pltpu.VMEM(block, BF16),
            pltpu.VMEM(block, F32),
            pltpu.VMEM(block, F32),
            pltpu.VMEM(block, F32),
            pltpu.VMEM(block, BF16),
            pltpu.VMEM(block, BF16),
            pltpu.VMEM((width, rows), BF16),
            pltpu.VMEM((width, rows), BF16),
            pltpu.VMEM((halves, parts, GROUP, LANES), BF16),
            pltpu.VMEM((halves, parts, GROUP, LANES), BF16),
            pltpu.VMEM((halves, parts, GROUP, LANES), BF16),
            pltpu.VMEM((width, rows), BF16),
            pltpu.VMEM((ROWS, 2 * LANES), BF16),
            pltpu.VMEM((ROWS, 2 * LANES), BF16),
            pltpu.VMEM((halves, ROWS, 2 * LANES), F32),
            pltpu.VMEM((ROWS, 2 * LANES), F32),
            pltpu.VMEM((rounds, 8, LANES), F32),
            pltpu.VMEM((8, LANES), F32),
            dma((10,)),
            dma((3,)),
            dma((3,)),
            dma((halves,)),
            dma((halves,)),
            dma((halves,)),
            dma((halves,)),
            dma((halves,)),
            dma,
            dma,
            dma,
            dma((2,)),
        ],
        compiler_params=pltpu.CompilerParams(
            collective_id=0, has_side_effects=True, vmem_limit_bytes=60 * 1024 * 1024
        ),
        cost_estimate=pl.CostEstimate(flops=2 * 10**9, bytes_accessed=2 * 10**6, transcendentals=0),
    )(
        queries, keys, values, filters, short_weight, skip_gain[None, :], residual, norm_gain[None, :],
        jnp.asarray(matrices), jnp.asarray(twist),
    )


def solution(mesh):
    placed = (
        P("seq", "ch"),
        P("seq", "ch"),
        P("seq", "ch"),
        P("seq", "ch"),
        P(None, None, "ch"),
        P("ch"),
        P("seq", "ch"),
        P("ch"),
    )
    return jax.shard_map(
        shards,
        mesh=mesh,
        in_specs=placed,
        out_specs=(P("seq", "ch"), P("seq", "ch")),
        check_vma=False,
    )
```

```python
import functools
import math

import jax
import jax.numpy as jnp
import numpy as np
from jax import lax
from jax.experimental import pallas as pl
from jax.experimental.pallas import tpu as pltpu
from jax.sharding import PartitionSpec as P

F32 = jnp.float32
BF16 = jnp.bfloat16
LANES = 128
GROUP = 16
PARTS = 32
ROOT = math.sqrt(0.5)

KEPT = (
    [0, 8, 16, 24, 32]
    + [1 + 8 * b for b in range(8)]
    + [2 + 8 * b for b in range(8)]
    + [3 + 8 * b for b in range(8)]
    + [4 + 8 * b for b in range(4)]
)
PLACE = {k1: i for i, k1 in enumerate(KEPT)}
ROWS = len(KEPT) * GROUP
CHUNK = 11 * GROUP


STEPS = sorted(
    ((dx, dy, dc) for dx in range(4) for dy in range(4) for dc in range(2) if dx + dy + dc > 0),
    key=lambda step: -(min(step[0], 4 - step[0]) + min(step[1], 4 - step[1])),
)


def tables():
    lane = np.arange(LANES)
    angle = 2.0 * np.pi * (np.outer(lane, lane) % LANES) / LANES
    cos, sin = np.cos(angle), np.sin(angle)
    forward = np.block([[cos, -sin], [sin, cos]])
    backward = np.block([[cos, sin], [-sin, cos]])
    parts = []
    for matrix in (forward, backward):
        high = matrix.astype(np.float32).astype(jnp.bfloat16)
        low = (matrix - high.astype(np.float64)).astype(np.float32).astype(jnp.bfloat16)
        parts += [high, low]
    matrices = np.stack(parts)
    turn = 2.0 * np.pi * np.outer(KEPT, lane) / (64 * LANES)
    weight = np.where(np.isin(KEPT, [0, 32]), 1.0, 2.0)[:, None] / (64 * LANES)
    twist = np.stack([np.cos(turn), -np.sin(turn), weight * np.cos(turn), weight * np.sin(turn)])
    return matrices, twist.astype(np.float32)


def plus(a, b):
    if a is None:
        return b
    return a if b is None else a + b


def neg(a):
    return None if a is None else -a


def minus(a, b):
    if b is None:
        return a
    return -b if a is None else a - b


def scaled(a, factor):
    return None if a is None else a * factor


def cplus(a, b):
    return (plus(a[0], b[0]), plus(a[1], b[1]))


def cminus(a, b):
    return (minus(a[0], b[0]), minus(a[1], b[1]))


def quarter(a, sign):
    return (neg(a[1]), a[0]) if sign > 0 else (a[1], neg(a[0]))


def turned(a, angle):
    cos, sin = math.cos(angle), math.sin(angle)
    if angle == 0.0:
        return a
    return (
        minus(scaled(a[0], cos), scaled(a[1], sin)),
        plus(scaled(a[1], cos), scaled(a[0], sin)),
    )


def dft4(z, sign):
    a, b = cplus(z[0], z[2]), cminus(z[0], z[2])
    c, d = cplus(z[1], z[3]), quarter(cminus(z[1], z[3]), sign)
    return [cplus(a, c), cplus(b, d), cminus(a, c), cminus(b, d)]


def dft8(z, sign):
    even, odd = dft4(z[0::2], sign), dft4(z[1::2], sign)
    a, b = odd[1], odd[3]
    if sign > 0:
        first = (scaled(minus(a[0], a[1]), ROOT), scaled(plus(a[0], a[1]), ROOT))
        third = (scaled(plus(b[0], b[1]), -ROOT), scaled(minus(b[0], b[1]), ROOT))
    else:
        first = (scaled(plus(a[0], a[1]), ROOT), scaled(minus(a[1], a[0]), ROOT))
        third = (scaled(minus(b[1], b[0]), ROOT), scaled(plus(b[0], b[1]), -ROOT))
    odd = [odd[0], first, quarter(odd[2], sign), third]
    return [cplus(e, o) for e, o in zip(even, odd)] + [cminus(e, o) for e, o in zip(even, odd)]


def forward64(x):
    column = [[None] * 8 for _ in range(5)]
    for s in range(8):
        x0, x1, x2, x3 = x[s], x[8 + s], x[16 + s], x[24 + s]
        a, b, c, d = x0 + x2, x1 + x3, x0 - x2, (x1 - x3)
        rb, rd = b * ROOT, d * ROOT
        values = [(a + b, None), (x0 + rd, -x2 - rb), (c, -d), (x0 - rd, x2 - rb), (a - b, None)]
        for k in range(5):
            column[k][s] = turned(values[k], -2.0 * math.pi * s * k / 64)
    out = {}
    for k in range(5):
        result = dft8(column[k], -1)
        for b in range((5, 8, 8, 8, 4)[k]):
            out[k + 8 * b] = result[b]
    return out


def backward64(get):
    v = []
    for k in range(5):
        count = (5, 8, 8, 8, 4)[k]
        z = [get(k + 8 * b) if b < count else (None, None) for b in range(8)]
        if k == 0:
            z[0], z[4] = (z[0][0], None), (z[4][0], None)
        u = dft8(z, 1)
        v.append([turned(u[s], 2.0 * math.pi * s * k / 64) for s in range(8)])
    y = [None] * 32
    for s in range(8):
        (a, _), (br, bi), (cr, ci), (dr, di), (e, _) = [v[k][s] for k in range(5)]
        p, m = a + e, a - e
        y[s] = (p + cr) + (br + dr)
        y[16 + s] = (p - cr) + (di - bi)
        f, g = (br - dr) * ROOT, (bi + di) * ROOT
        y[8 + s] = (m - ci) + (f - g)
        y[24 + s] = (m + ci) - (f + g)
    return y


def split(a):
    high = a.astype(BF16)
    return high, (a - high.astype(F32)).astype(BF16)


def product3(high, low, matrix_high, matrix_low):
    dot = functools.partial(jnp.dot, preferred_element_type=F32)
    return dot(high, matrix_high) + (dot(low, matrix_high) + dot(high, matrix_low))


def kernel(
    queries, keys, values, filters, short_taps, skip, residual, gain, matrices, twist,
    total_f, scale_v, gain_v,
    q_in, k_in, v_in, f_in, r_in, short_weight, skip_gain, mat, tw, tail_kv, halo, ext, mixed, short_q, base,
    send_f, send_m, got_f, got_m, send_y, got_y, a_high, a_low, spec_f, back, sums, own_sum,
    in_sem, halo_send, halo_recv, f_send, f_recv, m_send, m_recv, y_send, y_recv, p_send, p_recv,
):
    parts, rounds = lax.axis_size("seq"), lax.axis_size("ch")
    me, plane = lax.axis_index("seq"), lax.axis_index("ch")
    rows, width = q_in.shape
    own = width // parts
    halves = own // GROUP
    blocks = width // LANES

    barrier = pltpu.get_barrier_semaphore()

    @pl.loop(1, parts)
    def _(d):
        pl.semaphore_signal(barrier, inc=1, device_id={"seq": lax.rem(me + d, parts)})

    @pl.loop(1, rounds)
    def _(d):
        pl.semaphore_signal(barrier, inc=1, device_id={"ch": lax.rem(plane + d, rounds)})

    loads = [
        pltpu.make_async_copy(source, target, in_sem.at[i])
        for i, (source, target) in enumerate(
            [
                (filters, f_in), (keys, k_in), (values, v_in), (queries, q_in), (residual, r_in),
                (short_taps, short_weight), (skip, skip_gain), (gain, gain_v),
                (matrices, mat), (twist, tw),
            ]
        )
    ]
    for load in loads:
        load.start()

    def lanes(b):
        return pl.ds(pl.multiple_of(b * LANES, LANES), LANES)

    loads[0].wait()

    @pl.loop(0, blocks)
    def _(b):
        send_f[lanes(b), :] = f_in[:, lanes(b)].astype(F32).T.astype(BF16)

    for i in (1, 2, 3):
        loads[i].wait()
    for i, stream in enumerate((q_in, k_in, v_in)):
        ext[i, pl.ds(8, rows), :] = stream[...].astype(F32)

    last = pl.ds(rows - GROUP, GROUP)
    tail_kv[...] = jnp.concatenate(
        [k_in[last, :].astype(F32)[8:], v_in[last, :].astype(F32)[8:]], axis=0
    ).astype(BF16)

    pl.semaphore_wait(barrier, parts - 1 + rounds - 1)

    after = {"seq": lax.rem(me + 1, parts)}
    tails = [
        pltpu.make_async_remote_copy(
            src_ref=source,
            dst_ref=halo.at[i],
            send_sem=halo_send.at[i],
            recv_sem=halo_recv.at[i],
            device_id=after,
        )
        for i, source in enumerate((tail_kv, q_in.at[pl.ds(rows - GROUP, GROUP), :]))
    ]
    tails[0].start()

    def own_rows(peer, h):
        return pl.ds(pl.multiple_of(peer * own + h * GROUP, GROUP), GROUP)

    x, y, core = me // 8, lax.rem(me // 2, 4), lax.rem(me, 2)
    peers = [
        lax.rem(x + dx, 4) * 8 + lax.rem(y + dy, 4) * 2 + lax.rem(core + dc, 2)
        for dx, dy, dc in STEPS
    ]

    def exchange(source, target, send_sem, recv_sem):
        pltpu.make_async_copy(source(me), target, recv_sem).start()
        for peer in peers:
            pltpu.make_async_remote_copy(
                src_ref=source(peer),
                dst_ref=target,
                send_sem=send_sem,
                recv_sem=recv_sem,
                device_id={"seq": peer},
            ).start()

    for h in range(halves):
        exchange(
            lambda peer: send_f.at[own_rows(peer, h)], got_f.at[h, me], f_send.at[h], f_recv.at[h]
        )

    tails[0].wait_recv()
    first = me == 0
    head = jnp.where(first, 0.0, halo[0].astype(F32))
    ext[1, pl.ds(0, 8), :] = head[:8]
    ext[2, pl.ds(0, 8), :] = head[8:]
    loads[5].wait()

    def short(i, b):
        weights = short_weight[i, :, lanes(b)].astype(F32)
        total = weights[0:1] * ext[i, pl.ds(8, rows), lanes(b)]
        for j in range(1, weights.shape[0]):
            total = total + weights[j : j + 1] * ext[i, pl.ds(8 - j, rows), lanes(b)]
        return total

    @pl.loop(0, blocks)
    def _(b):
        product = (short(1, b) * short(2, b)).astype(BF16)
        mixed[:, lanes(b)] = product
        send_m[lanes(b), :] = product.astype(F32).T.astype(BF16)

    for h in range(halves):
        exchange(
            lambda peer: send_m.at[own_rows(peer, h)], got_m.at[h, me], m_send.at[h], m_recv.at[h]
        )

    tails[1].start()
    tails[1].wait_recv()
    ext[0, pl.ds(0, 8), :] = jnp.where(first, 0.0, halo[1].astype(F32))[8:]
    loads[4].wait()
    loads[6].wait()

    @pl.loop(0, blocks)
    def _(b):
        gate = short(0, b)
        short_q[:, lanes(b)] = gate
        direct = skip_gain[:, lanes(b)] * mixed[:, lanes(b)].astype(F32)
        base[:, lanes(b)] = r_in[:, lanes(b)].astype(F32) + gate * direct

    loads[8].wait()
    loads[9].wait()

    def twisted(value, i, which):
        cos, sin = tw[which, pl.ds(i, 1), :], tw[which + 1, pl.ds(i, 1), :]
        if value[1] is None:
            return value[0] * cos, value[0] * sin
        return value[0] * cos - value[1] * sin, value[1] * cos + value[0] * sin

    def first_stage(got, h):
        spectrum = forward64([got[h, s].astype(F32) for s in range(PARTS)])
        for k1 in KEPT:
            i = PLACE[k1]
            for half, part in enumerate(twisted(spectrum[k1], i, 0)):
                high, low = split(part)
                place = (pl.ds(i * GROUP, GROUP), pl.ds(half * LANES, LANES))
                a_high[place] = high
                a_low[place] = low

    for h in range(halves):
        pltpu.make_async_copy(got_f.at[h], got_f.at[h], f_recv.at[h]).wait()

    @pl.loop(0, halves)
    def _(h):
        first_stage(got_f, h)
        for c in range(ROWS // CHUNK):
            chunk = pl.ds(c * CHUNK, CHUNK)
            spec_f[h, chunk, :] = product3(a_high[chunk, :], a_low[chunk, :], mat[0], mat[1])

    @pl.loop(0, halves)
    def _(h):
        pass
        pltpu.make_async_copy(got_m.at[h], got_m.at[h], m_recv.at[h]).wait()
        first_stage(got_m, h)
        for c in range(ROWS // CHUNK):
            chunk = pl.ds(c * CHUNK, CHUNK)
            signal = product3(a_high[chunk, :], a_low[chunk, :], mat[0], mat[1])
            taps = spec_f[h, chunk, :]
            sr, si = signal[:, :LANES], signal[:, LANES:]
            fr, fi = taps[:, :LANES], taps[:, LANES:]
            both = jnp.concatenate([sr * fr - si * fi, sr * fi + si * fr], axis=1)
            high, low = split(both)
            back[chunk, :] = product3(high, low, mat[2], mat[3])

        def value(k1):
            i = PLACE[k1]
            part = pl.ds(i * GROUP, GROUP)
            return twisted((back[part, pl.ds(0, LANES)], back[part, pl.ds(LANES, LANES)]), i, 2)

        for s, y in enumerate(backward64(value)):
            send_y[h, s] = y.astype(BF16)
        exchange(lambda peer: send_y.at[h, peer], got_y.at[own_rows(me, h)], y_send.at[h], y_recv)

    pltpu.make_async_copy(got_y, got_y, y_recv).wait()

    partial = jnp.zeros((rows, LANES), F32)
    for b in range(blocks):
        at = pl.ds(b * LANES, LANES)
        conv = got_y[at, :].astype(F32).T
        total = base[:, at] + short_q[:, at] * conv
        value = total.astype(BF16).astype(F32)
        total_f[:, at] = value
        partial = partial + value * value
    own_sum[...] = jnp.broadcast_to(jnp.sum(partial.T, axis=0, keepdims=True), own_sum.shape)
    pltpu.make_async_copy(own_sum, sums.at[plane], p_recv).start()

    for d in sorted(range(1, rounds), key=lambda d: -min(d, rounds - d)):
        pltpu.make_async_remote_copy(
            src_ref=own_sum,
            dst_ref=sums.at[plane],
            send_sem=p_send,
            recv_sem=p_recv,
            device_id={"ch": lax.rem(plane + d, rounds)},
        ).start()

    pltpu.make_async_copy(sums, sums, p_recv).wait()
    power = jnp.sum(sums[...], axis=0)[0:1] / (width * rounds)
    loads[7].wait()
    scale_v[...] = lax.rsqrt(power + 1e-05)

    for copy in tails:
        copy.wait_send()
    others = pl.ds(0, parts - 1)
    for h in range(halves):
        pass
        pltpu.make_async_copy(got_f.at[h, others], got_f.at[h, others], f_send.at[h]).wait()
        pltpu.make_async_copy(got_m.at[h, others], got_m.at[h, others], m_send.at[h]).wait()
        pltpu.make_async_copy(got_m.at[h, others], got_m.at[h, others], y_send.at[h]).wait()
    if rounds > 1:
        most = sums.at[pl.ds(0, rounds - 1)]
        pltpu.make_async_copy(most, most, p_send).wait()


def shards(queries, keys, values, filters, short_weight, skip_gain, residual, norm_gain):
    rows, width = queries.shape
    parts, rounds = lax.axis_size("seq"), lax.axis_size("ch")
    taps = short_weight.shape[1]
    own = width // parts
    halves = own // GROUP
    assert parts == PARTS and rows == LANES and own % GROUP == 0
    matrices, twist = tables()
    block = (rows, width)
    whole = pl.BlockSpec(memory_space=pltpu.HBM)
    near = pl.BlockSpec(memory_space=pltpu.VMEM)
    dma = pltpu.SemaphoreType.DMA
    fixed = lambda a: pltpu.with_memory_space_constraint(a, pltpu.HBM)
    total, scale, gain = pl.pallas_call(
        kernel,
        out_shape=(jax.ShapeDtypeStruct(block, F32), jax.ShapeDtypeStruct((1, rows), F32), jax.ShapeDtypeStruct((1, width), F32)),
        in_specs=[whole] * 10,
        out_specs=(near, near, near),
        scratch_shapes=[
            pltpu.VMEM(block, BF16),
            pltpu.VMEM(block, BF16),
            pltpu.VMEM(block, BF16),
            pltpu.VMEM(block, BF16),
            pltpu.VMEM(block, BF16),
            pltpu.VMEM((3, taps, width), BF16),
            pltpu.VMEM((1, width), F32),
            pltpu.VMEM(matrices.shape, BF16),
            pltpu.VMEM(twist.shape, F32),
            pltpu.VMEM((GROUP, width), BF16),
            pltpu.VMEM((2, GROUP, width), BF16),
            pltpu.VMEM((3, rows + 8, width), F32),
            pltpu.VMEM(block, BF16),
            pltpu.VMEM(block, F32),
            pltpu.VMEM(block, F32),
            pltpu.VMEM((width, rows), BF16),
            pltpu.VMEM((width, rows), BF16),
            pltpu.VMEM((halves, parts, GROUP, LANES), BF16),
            pltpu.VMEM((halves, parts, GROUP, LANES), BF16),
            pltpu.VMEM((halves, parts, GROUP, LANES), BF16),
            pltpu.VMEM((width, rows), BF16),
            pltpu.VMEM((ROWS, 2 * LANES), BF16),
            pltpu.VMEM((ROWS, 2 * LANES), BF16),
            pltpu.VMEM((halves, ROWS, 2 * LANES), F32),
            pltpu.VMEM((ROWS, 2 * LANES), F32),
            pltpu.VMEM((rounds, 8, LANES), F32),
            pltpu.VMEM((8, LANES), F32),
            dma((10,)),
            dma((2,)),
            dma((2,)),
            dma((halves,)),
            dma((halves,)),
            dma((halves,)),
            dma((halves,)),
            dma((halves,)),
            dma,
            dma,
            dma,
        ],
        compiler_params=pltpu.CompilerParams(
            collective_id=0, has_side_effects=True, vmem_limit_bytes=32 * 1024 * 1024
        ),
        cost_estimate=pl.CostEstimate(flops=2 * 10**9, bytes_accessed=2 * 10**6, transcendentals=0),
    )(
        *[
            fixed(a)
            for a in (
                queries, keys, values, filters, short_weight, skip_gain[None, :], residual, norm_gain[None, :],
                jnp.asarray(matrices), jnp.asarray(twist),
            )
        ]
    )
    stream_out = total.astype(BF16)
    normed = (stream_out.astype(F32) * scale[0][:, None] * gain[0]).astype(BF16)
    return stream_out, normed


def solution(mesh):
    placed = (
        P("seq", "ch"),
        P("seq", "ch"),
        P("seq", "ch"),
        P("seq", "ch"),
        P(None, None, "ch"),
        P("ch"),
        P("seq", "ch"),
        P("ch"),
    )
    return jax.shard_map(
        shards,
        mesh=mesh,
        in_specs=placed,
        out_specs=(P("seq", "ch"), P("seq", "ch")),
        check_vma=False,
    )
```

```python
import functools
import math

import jax
import jax.numpy as jnp
import numpy as np
from jax import lax
from jax.experimental import pallas as pl
from jax.experimental.pallas import tpu as pltpu
from jax.sharding import PartitionSpec as P

F32 = jnp.float32
BF16 = jnp.bfloat16
LANES = 128
GROUP = 16
PARTS = 32
ROOT = math.sqrt(0.5)

KEPT = (
    [0, 8, 16, 24, 32]
    + [1 + 8 * b for b in range(8)]
    + [2 + 8 * b for b in range(8)]
    + [3 + 8 * b for b in range(8)]
    + [4 + 8 * b for b in range(4)]
)
PLACE = {k1: i for i, k1 in enumerate(KEPT)}
ROWS = len(KEPT) * GROUP
CHUNK = 11 * GROUP


STEPS = sorted(
    ((dx, dy, dc) for dx in range(4) for dy in range(4) for dc in range(2) if dx + dy + dc > 0),
    key=lambda step: -(min(step[0], 4 - step[0]) + min(step[1], 4 - step[1])),
)


def tables():
    lane = np.arange(LANES)
    angle = 2.0 * np.pi * (np.outer(lane, lane) % LANES) / LANES
    cos, sin = np.cos(angle), np.sin(angle)
    forward = np.block([[cos, -sin], [sin, cos]])
    backward = np.block([[cos, sin], [-sin, cos]])
    parts = []
    for matrix in (forward, backward):
        high = matrix.astype(np.float32).astype(jnp.bfloat16)
        low = (matrix - high.astype(np.float64)).astype(np.float32).astype(jnp.bfloat16)
        parts += [high, low]
    matrices = np.stack(parts)
    turn = 2.0 * np.pi * np.outer(KEPT, lane) / (64 * LANES)
    weight = np.where(np.isin(KEPT, [0, 32]), 1.0, 2.0)[:, None] / (64 * LANES)
    twist = np.stack([np.cos(turn), -np.sin(turn), weight * np.cos(turn), weight * np.sin(turn)])
    return matrices, twist.astype(np.float32)


def plus(a, b):
    if a is None:
        return b
    return a if b is None else a + b


def neg(a):
    return None if a is None else -a


def minus(a, b):
    if b is None:
        return a
    return -b if a is None else a - b


def scaled(a, factor):
    return None if a is None else a * factor


def cplus(a, b):
    return (plus(a[0], b[0]), plus(a[1], b[1]))


def cminus(a, b):
    return (minus(a[0], b[0]), minus(a[1], b[1]))


def quarter(a, sign):
    return (neg(a[1]), a[0]) if sign > 0 else (a[1], neg(a[0]))


def turned(a, angle):
    cos, sin = math.cos(angle), math.sin(angle)
    if angle == 0.0:
        return a
    return (
        minus(scaled(a[0], cos), scaled(a[1], sin)),
        plus(scaled(a[1], cos), scaled(a[0], sin)),
    )


def dft4(z, sign):
    a, b = cplus(z[0], z[2]), cminus(z[0], z[2])
    c, d = cplus(z[1], z[3]), quarter(cminus(z[1], z[3]), sign)
    return [cplus(a, c), cplus(b, d), cminus(a, c), cminus(b, d)]


def dft8(z, sign):
    even, odd = dft4(z[0::2], sign), dft4(z[1::2], sign)
    a, b = odd[1], odd[3]
    if sign > 0:
        first = (scaled(minus(a[0], a[1]), ROOT), scaled(plus(a[0], a[1]), ROOT))
        third = (scaled(plus(b[0], b[1]), -ROOT), scaled(minus(b[0], b[1]), ROOT))
    else:
        first = (scaled(plus(a[0], a[1]), ROOT), scaled(minus(a[1], a[0]), ROOT))
        third = (scaled(minus(b[1], b[0]), ROOT), scaled(plus(b[0], b[1]), -ROOT))
    odd = [odd[0], first, quarter(odd[2], sign), third]
    return [cplus(e, o) for e, o in zip(even, odd)] + [cminus(e, o) for e, o in zip(even, odd)]


def forward64(x):
    column = [[None] * 8 for _ in range(5)]
    for s in range(8):
        x0, x1, x2, x3 = x[s], x[8 + s], x[16 + s], x[24 + s]
        a, b, c, d = x0 + x2, x1 + x3, x0 - x2, (x1 - x3)
        rb, rd = b * ROOT, d * ROOT
        values = [(a + b, None), (x0 + rd, -x2 - rb), (c, -d), (x0 - rd, x2 - rb), (a - b, None)]
        for k in range(5):
            column[k][s] = turned(values[k], -2.0 * math.pi * s * k / 64)
    out = {}
    for k in range(5):
        result = dft8(column[k], -1)
        for b in range((5, 8, 8, 8, 4)[k]):
            out[k + 8 * b] = result[b]
    return out


def backward64(get):
    v = []
    for k in range(5):
        count = (5, 8, 8, 8, 4)[k]
        z = [get(k + 8 * b) if b < count else (None, None) for b in range(8)]
        if k == 0:
            z[0], z[4] = (z[0][0], None), (z[4][0], None)
        u = dft8(z, 1)
        v.append([turned(u[s], 2.0 * math.pi * s * k / 64) for s in range(8)])
    y = [None] * 32
    for s in range(8):
        (a, _), (br, bi), (cr, ci), (dr, di), (e, _) = [v[k][s] for k in range(5)]
        p, m = a + e, a - e
        y[s] = (p + cr) + (br + dr)
        y[16 + s] = (p - cr) + (di - bi)
        f, g = (br - dr) * ROOT, (bi + di) * ROOT
        y[8 + s] = (m - ci) + (f - g)
        y[24 + s] = (m + ci) - (f + g)
    return y


def split(a):
    high = a.astype(BF16)
    return high, (a - high.astype(F32)).astype(BF16)


def product3(high, low, matrix_high, matrix_low):
    dot = functools.partial(jnp.dot, preferred_element_type=F32)
    return dot(high, matrix_high) + (dot(low, matrix_high) + dot(high, matrix_low))


def kernel(
    queries, keys, values, filters, short_taps, skip, residual, gain, matrices, twist,
    total_f, scale_v, gain_v,
    q_in, k_in, v_in, f_in, r_in, short_weight, skip_gain, mat, tw, tail_kv, halo, ext, mixed, short_q, base,
    send_f, send_m, got_f, got_m, send_y, got_y, a_high, a_low, spec_f, back, sums, own_sum,
    in_sem, halo_send, halo_recv, f_send, f_recv, m_send, m_recv, y_send, y_recv, p_send, p_recv,
):
    parts, rounds = lax.axis_size("seq"), lax.axis_size("ch")
    me, plane = lax.axis_index("seq"), lax.axis_index("ch")
    rows, width = q_in.shape
    own = width // parts
    halves = own // GROUP
    blocks = width // LANES

    barrier = pltpu.get_barrier_semaphore()

    x, y, core = me // 8, lax.rem(me // 2, 4), lax.rem(me, 2)
    peers = [
        lax.rem(x + dx, 4) * 8 + lax.rem(y + dy, 4) * 2 + lax.rem(core + dc, 2)
        for dx, dy, dc in STEPS
    ]
    for peer in peers:
        pl.semaphore_signal(barrier, inc=1, device_id={"seq": peer})

    @pl.loop(1, rounds)
    def _(d):
        pl.semaphore_signal(barrier, inc=1, device_id={"ch": lax.rem(plane + d, rounds)})

    loads = [
        pltpu.make_async_copy(source, target, in_sem.at[i])
        for i, (source, target) in enumerate(
            [
                (filters, f_in), (keys, k_in), (values, v_in), (queries, q_in), (residual, r_in),
                (short_taps, short_weight), (skip, skip_gain), (gain, gain_v),
                (matrices, mat), (twist, tw),
            ]
        )
    ]
    for load in loads:
        load.start()

    def lanes(b):
        return pl.ds(pl.multiple_of(b * LANES, LANES), LANES)

    loads[0].wait()

    @pl.loop(0, blocks)
    def _(b):
        send_f[lanes(b), :] = f_in[:, lanes(b)].T

    for i in (1, 2, 3):
        loads[i].wait()
    for i, stream in enumerate((q_in, k_in, v_in)):
        ext[i, pl.ds(8, rows), :] = stream[...].astype(F32)

    last = pl.ds(rows - GROUP, GROUP)
    tail_kv[...] = jnp.concatenate(
        [k_in[last, :].astype(F32)[8:], v_in[last, :].astype(F32)[8:]], axis=0
    ).astype(BF16)

    pl.semaphore_wait(barrier, parts - 1 + rounds - 1)

    after = {"seq": lax.rem(me + 1, parts)}
    tails = [
        pltpu.make_async_remote_copy(
            src_ref=source,
            dst_ref=halo.at[i],
            send_sem=halo_send.at[i],
            recv_sem=halo_recv.at[i],
            device_id=after,
        )
        for i, source in enumerate((tail_kv, q_in.at[pl.ds(rows - GROUP, GROUP), :]))
    ]
    tails[0].start()

    def own_rows(peer, h):
        return pl.ds(pl.multiple_of(peer * own + h * GROUP, GROUP), GROUP)

    def exchange(source, target, send_sem, recv_sem):
        pltpu.make_async_copy(source(me), target, recv_sem).start()
        for peer in peers:
            pltpu.make_async_remote_copy(
                src_ref=source(peer),
                dst_ref=target,
                send_sem=send_sem,
                recv_sem=recv_sem,
                device_id={"seq": peer},
            ).start()

    for h in range(halves):
        exchange(
            lambda peer: send_f.at[own_rows(peer, h)], got_f.at[h, me], f_send.at[h], f_recv.at[h]
        )

    def short(i, b, count):
        weights = short_weight[i, :, lanes(b)].astype(F32)
        total = weights[0:1] * ext[i, pl.ds(8, count), lanes(b)]
        for j in range(1, weights.shape[0]):
            total = total + weights[j : j + 1] * ext[i, pl.ds(8 - j, count), lanes(b)]
        return total

    loads[5].wait()
    for i in range(3):
        ext[i, pl.ds(0, 8), :] = jnp.zeros((8, width), F32)

    @pl.loop(0, blocks)
    def _(b):
        product = short(1, b, rows) * short(2, b, rows)
        mixed[:, lanes(b)] = product.astype(BF16)
        send_m[lanes(b), :] = product.astype(BF16).T

    tails[0].wait_recv()
    first = me == 0
    head = jnp.where(first, 0.0, halo[0].astype(F32))
    ext[1, pl.ds(0, 8), :] = head[:8]
    ext[2, pl.ds(0, 8), :] = head[8:]

    @pl.loop(0, blocks)
    def _(b):
        product = short(1, b, GROUP) * short(2, b, GROUP)
        mixed[pl.ds(0, GROUP), lanes(b)] = product.astype(BF16)
        send_m[lanes(b), pl.ds(0, GROUP)] = product.astype(BF16).T

    for h in range(halves):
        exchange(
            lambda peer: send_m.at[own_rows(peer, h)], got_m.at[h, me], m_send.at[h], m_recv.at[h]
        )

    tails[1].start()
    loads[8].wait()
    loads[9].wait()

    def twisted(value, i, which):
        cos, sin = tw[which, pl.ds(i, 1), :], tw[which + 1, pl.ds(i, 1), :]
        if value[1] is None:
            return value[0] * cos, value[0] * sin
        return value[0] * cos - value[1] * sin, value[1] * cos + value[0] * sin

    def first_stage(got, h):
        spectrum = forward64([got[h, s].astype(F32) for s in range(PARTS)])
        for k1 in KEPT:
            i = PLACE[k1]
            for half, part in enumerate(twisted(spectrum[k1], i, 0)):
                high, low = split(part)
                place = (pl.ds(i * GROUP, GROUP), pl.ds(half * LANES, LANES))
                a_high[place] = high
                a_low[place] = low

    for h in range(halves):
        pltpu.make_async_copy(got_f.at[h], got_f.at[h], f_recv.at[h]).wait()

    @pl.loop(0, halves)
    def _(h):
        first_stage(got_f, h)
        for c in range(ROWS // CHUNK):
            chunk = pl.ds(c * CHUNK, CHUNK)
            spec_f[h, chunk, :] = product3(a_high[chunk, :], a_low[chunk, :], mat[0], mat[1])

    @pl.loop(0, halves)
    def _(h):
        pass
        pltpu.make_async_copy(got_m.at[h], got_m.at[h], m_recv.at[h]).wait()
        first_stage(got_m, h)
        for c in range(ROWS // CHUNK):
            chunk = pl.ds(c * CHUNK, CHUNK)
            signal = product3(a_high[chunk, :], a_low[chunk, :], mat[0], mat[1])
            taps = spec_f[h, chunk, :]
            sr, si = signal[:, :LANES], signal[:, LANES:]
            fr, fi = taps[:, :LANES], taps[:, LANES:]
            both = jnp.concatenate([sr * fr - si * fi, sr * fi + si * fr], axis=1)
            high, low = split(both)
            back[chunk, :] = product3(high, low, mat[2], mat[3])

        def value(k1):
            i = PLACE[k1]
            part = pl.ds(i * GROUP, GROUP)
            return twisted((back[part, pl.ds(0, LANES)], back[part, pl.ds(LANES, LANES)]), i, 2)

        for s, y in enumerate(backward64(value)):
            send_y[h, s] = y.astype(BF16)
        exchange(lambda peer: send_y.at[h, peer], got_y.at[own_rows(me, h)], y_send.at[h], y_recv)

    tails[1].wait_recv()
    ext[0, pl.ds(0, 8), :] = jnp.where(first, 0.0, halo[1].astype(F32))[8:]
    loads[4].wait()
    loads[6].wait()

    @pl.loop(0, blocks)
    def _(b):
        gate = short(0, b, rows)
        short_q[:, lanes(b)] = gate
        direct = skip_gain[:, lanes(b)] * mixed[:, lanes(b)].astype(F32)
        base[:, lanes(b)] = r_in[:, lanes(b)].astype(F32) + gate * direct

    pltpu.make_async_copy(got_y, got_y, y_recv).wait()

    partial = jnp.zeros((rows, LANES), F32)
    for b in range(blocks):
        at = pl.ds(b * LANES, LANES)
        conv = got_y[at, :].T.astype(F32)
        total = base[:, at] + short_q[:, at] * conv
        value = total.astype(BF16).astype(F32)
        total_f[:, at] = value
        partial = partial + value * value
    own_sum[...] = jnp.broadcast_to(jnp.sum(partial.T, axis=0, keepdims=True), own_sum.shape)
    pltpu.make_async_copy(own_sum, sums.at[plane], p_recv).start()

    for d in sorted(range(1, rounds), key=lambda d: -min(d, rounds - d)):
        pltpu.make_async_remote_copy(
            src_ref=own_sum,
            dst_ref=sums.at[plane],
            send_sem=p_send,
            recv_sem=p_recv,
            device_id={"ch": lax.rem(plane + d, rounds)},
        ).start()

    pltpu.make_async_copy(sums, sums, p_recv).wait()
    power = jnp.sum(sums[...], axis=0)[0:1] / (width * rounds)
    loads[7].wait()
    scale_v[...] = lax.rsqrt(power + 1e-05)

    for copy in tails:
        copy.wait_send()
    others = pl.ds(0, parts - 1)
    for h in range(halves):
        pass
        pltpu.make_async_copy(got_f.at[h, others], got_f.at[h, others], f_send.at[h]).wait()
        pltpu.make_async_copy(got_m.at[h, others], got_m.at[h, others], m_send.at[h]).wait()
        pltpu.make_async_copy(got_m.at[h, others], got_m.at[h, others], y_send.at[h]).wait()
    if rounds > 1:
        most = sums.at[pl.ds(0, rounds - 1)]
        pltpu.make_async_copy(most, most, p_send).wait()


def shards(queries, keys, values, filters, short_weight, skip_gain, residual, norm_gain):
    rows, width = queries.shape
    parts, rounds = lax.axis_size("seq"), lax.axis_size("ch")
    taps = short_weight.shape[1]
    own = width // parts
    halves = own // GROUP
    assert parts == PARTS and rows == LANES and own % GROUP == 0
    matrices, twist = tables()
    block = (rows, width)
    whole = pl.BlockSpec(memory_space=pltpu.HBM)
    near = pl.BlockSpec(memory_space=pltpu.VMEM)
    dma = pltpu.SemaphoreType.DMA
    fixed = lambda a: pltpu.with_memory_space_constraint(a, pltpu.HBM)
    total, scale, gain = pl.pallas_call(
        kernel,
        out_shape=(jax.ShapeDtypeStruct(block, F32), jax.ShapeDtypeStruct((1, rows), F32), jax.ShapeDtypeStruct((1, width), F32)),
        in_specs=[whole] * 10,
        out_specs=(near, near, near),
        scratch_shapes=[
            pltpu.VMEM(block, BF16),
            pltpu.VMEM(block, BF16),
            pltpu.VMEM(block, BF16),
            pltpu.VMEM(block, BF16),
            pltpu.VMEM(block, BF16),
            pltpu.VMEM((3, taps, width), BF16),
            pltpu.VMEM((1, width), F32),
            pltpu.VMEM(matrices.shape, BF16),
            pltpu.VMEM(twist.shape, F32),
            pltpu.VMEM((GROUP, width), BF16),
            pltpu.VMEM((2, GROUP, width), BF16),
            pltpu.VMEM((3, rows + 8, width), F32),
            pltpu.VMEM(block, BF16),
            pltpu.VMEM(block, F32),
            pltpu.VMEM(block, F32),
            pltpu.VMEM((width, rows), BF16),
            pltpu.VMEM((width, rows), BF16),
            pltpu.VMEM((halves, parts, GROUP, LANES), BF16),
            pltpu.VMEM((halves, parts, GROUP, LANES), BF16),
            pltpu.VMEM((halves, parts, GROUP, LANES), BF16),
            pltpu.VMEM((width, rows), BF16),
            pltpu.VMEM((ROWS, 2 * LANES), BF16),
            pltpu.VMEM((ROWS, 2 * LANES), BF16),
            pltpu.VMEM((halves, ROWS, 2 * LANES), F32),
            pltpu.VMEM((ROWS, 2 * LANES), F32),
            pltpu.VMEM((rounds, 8, LANES), F32),
            pltpu.VMEM((8, LANES), F32),
            dma((10,)),
            dma((2,)),
            dma((2,)),
            dma((halves,)),
            dma((halves,)),
            dma((halves,)),
            dma((halves,)),
            dma((halves,)),
            dma,
            dma,
            dma,
        ],
        compiler_params=pltpu.CompilerParams(
            collective_id=0, has_side_effects=True, vmem_limit_bytes=32 * 1024 * 1024
        ),
        cost_estimate=pl.CostEstimate(flops=2 * 10**9, bytes_accessed=2 * 10**6, transcendentals=0),
    )(
        *[
            fixed(a)
            for a in (
                queries, keys, values, filters, short_weight, skip_gain[None, :], residual, norm_gain[None, :],
                jnp.asarray(matrices), jnp.asarray(twist),
            )
        ]
    )
    stream_out = total.astype(BF16)
    normed = (stream_out.astype(F32) * scale[0][:, None] * gain[0]).astype(BF16)
    return stream_out, normed


def solution(mesh):
    placed = (
        P("seq", "ch"),
        P("seq", "ch"),
        P("seq", "ch"),
        P("seq", "ch"),
        P(None, None, "ch"),
        P("ch"),
        P("seq", "ch"),
        P("ch"),
    )
    return jax.shard_map(
        shards,
        mesh=mesh,
        in_specs=placed,
        out_specs=(P("seq", "ch"), P("seq", "ch")),
        check_vma=False,
    )
```

```python
import functools
import math

import jax
import jax.numpy as jnp
import numpy as np
from jax import lax
from jax.experimental import pallas as pl
from jax.experimental.pallas import tpu as pltpu
from jax.sharding import PartitionSpec as P

F32 = jnp.float32
BF16 = jnp.bfloat16
LANES = 128
GROUP = 16
PARTS = 32
ROOT = math.sqrt(0.5)

KEPT = (
    [0, 8, 16, 24, 32]
    + [1 + 8 * b for b in range(8)]
    + [2 + 8 * b for b in range(8)]
    + [3 + 8 * b for b in range(8)]
    + [4 + 8 * b for b in range(4)]
)
PLACE = {k1: i for i, k1 in enumerate(KEPT)}
ROWS = len(KEPT) * GROUP
CHUNK = 11 * GROUP


STEPS = sorted(
    ((dx, dy, dc) for dx in range(4) for dy in range(4) for dc in range(2) if dx + dy + dc > 0),
    key=lambda step: -(min(step[0], 4 - step[0]) + min(step[1], 4 - step[1])),
)


ABS = sorted(range(32), key=lambda p: (p // 8 + p // 2 % 4, -(p % 2)))


def tables():
    lane = np.arange(LANES)
    angle = 2.0 * np.pi * (np.outer(lane, lane) % LANES) / LANES
    cos, sin = np.cos(angle), np.sin(angle)
    forward = np.block([[cos, -sin], [sin, cos]])
    backward = np.block([[cos, sin], [-sin, cos]])
    parts = []
    for matrix in (forward, backward):
        high = matrix.astype(np.float32).astype(jnp.bfloat16)
        low = (matrix - high.astype(np.float64)).astype(np.float32).astype(jnp.bfloat16)
        parts += [high, low]
    matrices = np.stack(parts[:3])
    turn = 2.0 * np.pi * np.outer(KEPT, lane) / (64 * LANES)
    weight = np.where(np.isin(KEPT, [0, 32]), 1.0, 2.0)[:, None] / (64 * LANES)
    twist = np.stack([np.cos(turn), -np.sin(turn), weight * np.cos(turn), weight * np.sin(turn)])
    return matrices, twist.astype(np.float32)


def plus(a, b):
    if a is None:
        return b
    return a if b is None else a + b


def neg(a):
    return None if a is None else -a


def minus(a, b):
    if b is None:
        return a
    return -b if a is None else a - b


def scaled(a, factor):
    return None if a is None else a * factor


def cplus(a, b):
    return (plus(a[0], b[0]), plus(a[1], b[1]))


def cminus(a, b):
    return (minus(a[0], b[0]), minus(a[1], b[1]))


def quarter(a, sign):
    return (neg(a[1]), a[0]) if sign > 0 else (a[1], neg(a[0]))


def turned(a, angle):
    cos, sin = math.cos(angle), math.sin(angle)
    if angle == 0.0:
        return a
    return (
        minus(scaled(a[0], cos), scaled(a[1], sin)),
        plus(scaled(a[1], cos), scaled(a[0], sin)),
    )


def dft4(z, sign):
    a, b = cplus(z[0], z[2]), cminus(z[0], z[2])
    c, d = cplus(z[1], z[3]), quarter(cminus(z[1], z[3]), sign)
    return [cplus(a, c), cplus(b, d), cminus(a, c), cminus(b, d)]


def dft8(z, sign):
    even, odd = dft4(z[0::2], sign), dft4(z[1::2], sign)
    a, b = odd[1], odd[3]
    if sign > 0:
        first = (scaled(minus(a[0], a[1]), ROOT), scaled(plus(a[0], a[1]), ROOT))
        third = (scaled(plus(b[0], b[1]), -ROOT), scaled(minus(b[0], b[1]), ROOT))
    else:
        first = (scaled(plus(a[0], a[1]), ROOT), scaled(minus(a[1], a[0]), ROOT))
        third = (scaled(minus(b[1], b[0]), ROOT), scaled(plus(b[0], b[1]), -ROOT))
    odd = [odd[0], first, quarter(odd[2], sign), third]
    return [cplus(e, o) for e, o in zip(even, odd)] + [cminus(e, o) for e, o in zip(even, odd)]


def forward64(x):
    column = [[None] * 8 for _ in range(5)]
    for s in range(8):
        x0, x1, x2, x3 = x[s], x[8 + s], x[16 + s], x[24 + s]
        a, b, c, d = x0 + x2, x1 + x3, x0 - x2, (x1 - x3)
        rb, rd = b * ROOT, d * ROOT
        values = [(a + b, None), (x0 + rd, -x2 - rb), (c, -d), (x0 - rd, x2 - rb), (a - b, None)]
        for k in range(5):
            column[k][s] = turned(values[k], -2.0 * math.pi * s * k / 64)
    out = {}
    for k in range(5):
        result = dft8(column[k], -1)
        for b in range((5, 8, 8, 8, 4)[k]):
            out[k + 8 * b] = result[b]
    return out


def backward64(get):
    v = []
    for k in range(5):
        count = (5, 8, 8, 8, 4)[k]
        z = [get(k + 8 * b) if b < count else (None, None) for b in range(8)]
        if k == 0:
            z[0], z[4] = (z[0][0], None), (z[4][0], None)
        u = dft8(z, 1)
        v.append([turned(u[s], 2.0 * math.pi * s * k / 64) for s in range(8)])
    y = [None] * 32
    for s in range(8):
        (a, _), (br, bi), (cr, ci), (dr, di), (e, _) = [v[k][s] for k in range(5)]
        p, m = a + e, a - e
        y[s] = (p + cr) + (br + dr)
        y[16 + s] = (p - cr) + (di - bi)
        f, g = (br - dr) * ROOT, (bi + di) * ROOT
        y[8 + s] = (m - ci) + (f - g)
        y[24 + s] = (m + ci) - (f + g)
    return y


def split(a):
    high = a.astype(BF16)
    return high, (a - high.astype(F32)).astype(BF16)


def matmul(a, matrix):
    return jnp.dot(a, matrix, preferred_element_type=F32)


def product3(high, low, matrix_high, matrix_low):
    return matmul(high, matrix_high) + (matmul(low, matrix_high) + matmul(high, matrix_low))


def kernel(
    queries, keys, values, filters, short_taps, skip, residual, gain, matrices, twist,
    total_f, scale_v, gain_v,
    q_in, k_in, v_in, f_in, r_in, short_weight, skip_gain, mat, tw, tail_kv, halo, ext, mixed, short_q, base,
    send_f, send_m, got_f, got_m, send_y, got_y, a_high, a_low, spec_f, back, sums, own_sum,
    in_sem, halo_send, halo_recv, f_send, f_recv, m_send, m_recv, y_send, y_recv, p_send, p_recv,
):
    parts, rounds = lax.axis_size("seq"), lax.axis_size("ch")
    me, plane = lax.axis_index("seq"), lax.axis_index("ch")
    rows, width = q_in.shape
    own = width // parts
    halves = own // GROUP
    blocks = width // LANES

    barrier = pltpu.get_barrier_semaphore()

    x, y, core = me // 8, lax.rem(me // 2, 4), lax.rem(me, 2)
    peers = [
        lax.rem(x + dx, 4) * 8 + lax.rem(y + dy, 4) * 2 + lax.rem(core + dc, 2)
        for dx, dy, dc in STEPS
    ]
    for peer in peers:
        pl.semaphore_signal(barrier, inc=1, device_id={"seq": peer})

    @pl.loop(1, rounds)
    def _(d):
        pl.semaphore_signal(barrier, inc=1, device_id={"ch": lax.rem(plane + d, rounds)})

    loads = [
        pltpu.make_async_copy(source, target, in_sem.at[i])
        for i, (source, target) in enumerate(
            [
                (filters, f_in), (keys, k_in), (values, v_in), (queries, q_in), (residual, r_in),
                (short_taps, short_weight), (skip, skip_gain), (gain, gain_v),
                (matrices, mat), (twist, tw),
            ]
        )
    ]
    for load in loads:
        load.start()

    def lanes(b):
        return pl.ds(pl.multiple_of(b * LANES, LANES), LANES)

    loads[0].wait()

    @pl.loop(0, blocks)
    def _(b):
        send_f[lanes(b), :] = f_in[:, lanes(b)].T

    for i in (1, 2, 3):
        loads[i].wait()
    last = pl.ds(rows - GROUP, GROUP)
    tail_kv[...] = jnp.concatenate(
        [k_in[last, :].astype(F32)[8:], v_in[last, :].astype(F32)[8:]], axis=0
    ).astype(BF16)

    pl.semaphore_wait(barrier, parts - 1 + rounds - 1)

    after = {"seq": lax.rem(me + 1, parts)}
    tails = [
        pltpu.make_async_remote_copy(
            src_ref=source,
            dst_ref=halo.at[i],
            send_sem=halo_send.at[i],
            recv_sem=halo_recv.at[i],
            device_id=after,
        )
        for i, source in enumerate((tail_kv, q_in.at[pl.ds(rows - GROUP, GROUP), :]))
    ]
    tails[0].start()

    def own_rows(peer, h):
        return pl.ds(pl.multiple_of(h * (width // halves) + peer * GROUP, GROUP), GROUP)

    def exchange_abs(source, target, send_sem, recv_sem):
        pltpu.make_async_copy(source(me), target, recv_sem).start()
        for peer in ABS:
            @pl.when(me != peer)
            def _():
                pltpu.make_async_remote_copy(
                    src_ref=source(peer),
                    dst_ref=target,
                    send_sem=send_sem,
                    recv_sem=recv_sem,
                    device_id={"seq": peer},
                ).start()

    def exchange(source, target, send_sem, recv_sem):
        pltpu.make_async_copy(source(me), target, recv_sem).start()
        for peer in peers:
            pltpu.make_async_remote_copy(
                src_ref=source(peer),
                dst_ref=target,
                send_sem=send_sem,
                recv_sem=recv_sem,
                device_id={"seq": peer},
            ).start()

    for h in range(halves):
        exchange(
            lambda peer: send_f.at[own_rows(peer, h)], got_f.at[h, me], f_send.at[h], f_recv.at[h]
        )

    for i, stream in enumerate((q_in, k_in, v_in)):
        ext[i, pl.ds(8, rows), :] = stream[...].astype(F32)

    def short(i, b, count):
        weights = short_weight[i, :, lanes(b)].astype(F32)
        total = weights[0:1] * ext[i, pl.ds(8, count), lanes(b)]
        for j in range(1, weights.shape[0]):
            total = total + weights[j : j + 1] * ext[i, pl.ds(8 - j, count), lanes(b)]
        return total

    loads[5].wait()
    for i in range(3):
        ext[i, pl.ds(0, 8), :] = jnp.zeros((8, width), F32)

    @pl.loop(0, blocks)
    def _(b):
        product = short(1, b, rows) * short(2, b, rows)
        mixed[:, lanes(b)] = product.astype(BF16)
        send_m[lanes(b), :] = product.astype(BF16).T

    tails[0].wait_recv()
    first = me == 0
    head = jnp.where(first, 0.0, halo[0].astype(F32))
    ext[1, pl.ds(0, 8), :] = head[:8]
    ext[2, pl.ds(0, 8), :] = head[8:]

    for h in range(halves):

        @pl.loop(h * blocks // halves, (h + 1) * blocks // halves)
        def _(b):
            product = short(1, b, GROUP) * short(2, b, GROUP)
            mixed[pl.ds(0, GROUP), lanes(b)] = product.astype(BF16)
            send_m[lanes(b), pl.ds(0, GROUP)] = product.astype(BF16).T

        exchange(
            lambda peer: send_m.at[own_rows(peer, h)], got_m.at[h, me], m_send.at[h], m_recv.at[h]
        )

    tails[1].start()
    loads[8].wait()
    loads[9].wait()

    def twisted(value, i, which):
        cos, sin = tw[which, pl.ds(i, 1), :], tw[which + 1, pl.ds(i, 1), :]
        if value[1] is None:
            return value[0] * cos, value[0] * sin
        return value[0] * cos - value[1] * sin, value[1] * cos + value[0] * sin

    def first_stage(got, h, low):
        spectrum = forward64([got[h, s].astype(F32) for s in range(PARTS)])
        for k1 in KEPT:
            i = PLACE[k1]
            for half, part in enumerate(twisted(spectrum[k1], i, 0)):
                place = (pl.ds(i * GROUP, GROUP), pl.ds(half * LANES, LANES))
                if low:
                    a_high[place], a_low[place] = split(part)
                else:
                    a_high[place] = part.astype(BF16)

    for h in range(halves):
        pltpu.make_async_copy(got_f.at[h], got_f.at[h], f_recv.at[h]).wait()

    @pl.loop(0, halves)
    def _(h):
        first_stage(got_f, h, True)
        for c in range(ROWS // CHUNK):
            chunk = pl.ds(c * CHUNK, CHUNK)
            spec_f[h, chunk, :] = product3(a_high[chunk, :], a_low[chunk, :], mat[0], mat[1])

    @pl.loop(0, halves)
    def _(h):
        pass
        pltpu.make_async_copy(got_m.at[h], got_m.at[h], m_recv.at[h]).wait()
        first_stage(got_m, h, False)
        for c in range(ROWS // CHUNK):
            chunk = pl.ds(c * CHUNK, CHUNK)
            signal = matmul(a_high[chunk, :], mat[0])
            taps = spec_f[h, chunk, :]
            sr, si = signal[:, :LANES], signal[:, LANES:]
            fr, fi = taps[:, :LANES], taps[:, LANES:]
            both = jnp.concatenate([sr * fr - si * fi, sr * fi + si * fr], axis=1)
            back[chunk, :] = matmul(both.astype(BF16), mat[2])

        def value(k1):
            i = PLACE[k1]
            part = pl.ds(i * GROUP, GROUP)
            return twisted((back[part, pl.ds(0, LANES)], back[part, pl.ds(LANES, LANES)]), i, 2)

        for s, y in enumerate(backward64(value)):
            send_y[h, s] = y.astype(BF16)
        exchange_abs(lambda peer: send_y.at[h, peer], got_y.at[own_rows(me, h)], y_send.at[h], y_recv.at[h])

    tails[1].wait_recv()
    ext[0, pl.ds(0, 8), :] = jnp.where(first, 0.0, halo[1].astype(F32))[8:]
    loads[4].wait()
    loads[6].wait()

    @pl.loop(0, blocks)
    def _(b):
        gate = short(0, b, rows)
        short_q[:, lanes(b)] = gate
        direct = skip_gain[:, lanes(b)] * mixed[:, lanes(b)].astype(F32)
        base[:, lanes(b)] = r_in[:, lanes(b)].astype(F32) + gate * direct

    partial = jnp.zeros((rows, LANES), F32)
    for h in range(halves):
        arrived = got_y.at[pl.ds(h * (width // halves), width // halves)]
        pltpu.make_async_copy(arrived, arrived, y_recv.at[h]).wait()
        for b in range(h * blocks // halves, (h + 1) * blocks // halves):
            at = pl.ds(b * LANES, LANES)
            conv = got_y[at, :].T.astype(F32)
            value = (base[:, at] + short_q[:, at] * conv).astype(BF16).astype(F32)
            total_f[:, at] = value
            partial = partial + value * value

    own_sum[...] = jnp.broadcast_to(jnp.sum(partial.T, axis=0, keepdims=True), own_sum.shape)
    pltpu.make_async_copy(own_sum, sums.at[plane], p_recv).start()

    for d in sorted(range(1, rounds), key=lambda d: -min(d, rounds - d)):
        pltpu.make_async_remote_copy(
            src_ref=own_sum,
            dst_ref=sums.at[plane],
            send_sem=p_send,
            recv_sem=p_recv,
            device_id={"ch": lax.rem(plane + d, rounds)},
        ).start()

    pltpu.make_async_copy(sums, sums, p_recv).wait()
    power = jnp.sum(sums[...], axis=0)[0:1] / (width * rounds)
    loads[7].wait()
    scale_v[...] = lax.rsqrt(power + 1e-05)

    for copy in tails:
        copy.wait_send()
    others = pl.ds(0, parts - 1)
    for h in range(halves):
        pass
        pltpu.make_async_copy(got_f.at[h, others], got_f.at[h, others], f_send.at[h]).wait()
        pltpu.make_async_copy(got_m.at[h, others], got_m.at[h, others], m_send.at[h]).wait()
        pltpu.make_async_copy(got_m.at[h, others], got_m.at[h, others], y_send.at[h]).wait()
    if rounds > 1:
        most = sums.at[pl.ds(0, rounds - 1)]
        pltpu.make_async_copy(most, most, p_send).wait()


def shards(queries, keys, values, filters, short_weight, skip_gain, residual, norm_gain):
    rows, width = queries.shape
    parts, rounds = lax.axis_size("seq"), lax.axis_size("ch")
    taps = short_weight.shape[1]
    own = width // parts
    halves = own // GROUP
    assert parts == PARTS and rows == LANES and own % GROUP == 0
    matrices, twist = tables()
    block = (rows, width)
    whole = pl.BlockSpec(memory_space=pltpu.HBM)
    near = pl.BlockSpec(memory_space=pltpu.VMEM)
    dma = pltpu.SemaphoreType.DMA
    fixed = lambda a: pltpu.with_memory_space_constraint(a, pltpu.HBM)
    total, scale, gain = pl.pallas_call(
        kernel,
        out_shape=(jax.ShapeDtypeStruct(block, F32), jax.ShapeDtypeStruct((1, rows), F32), jax.ShapeDtypeStruct((1, width), F32)),
        in_specs=[whole] * 10,
        out_specs=(near, near, near),
        scratch_shapes=[
            pltpu.VMEM(block, BF16),
            pltpu.VMEM(block, BF16),
            pltpu.VMEM(block, BF16),
            pltpu.VMEM(block, BF16),
            pltpu.VMEM(block, BF16),
            pltpu.VMEM((3, taps, width), BF16),
            pltpu.VMEM((1, width), F32),
            pltpu.VMEM(matrices.shape, BF16),
            pltpu.VMEM(twist.shape, F32),
            pltpu.VMEM((GROUP, width), BF16),
            pltpu.VMEM((2, GROUP, width), BF16),
            pltpu.VMEM((3, rows + 8, width), F32),
            pltpu.VMEM(block, BF16),
            pltpu.VMEM(block, F32),
            pltpu.VMEM(block, F32),
            pltpu.VMEM((width, rows), BF16),
            pltpu.VMEM((width, rows), BF16),
            pltpu.VMEM((halves, parts, GROUP, LANES), BF16),
            pltpu.VMEM((halves, parts, GROUP, LANES), BF16),
            pltpu.VMEM((halves, parts, GROUP, LANES), BF16),
            pltpu.VMEM((width, rows), BF16),
            pltpu.VMEM((ROWS, 2 * LANES), BF16),
            pltpu.VMEM((ROWS, 2 * LANES), BF16),
            pltpu.VMEM((halves, ROWS, 2 * LANES), F32),
            pltpu.VMEM((ROWS, 2 * LANES), F32),
            pltpu.VMEM((rounds, 8, LANES), F32),
            pltpu.VMEM((8, LANES), F32),
            dma((10,)),
            dma((2,)),
            dma((2,)),
            dma((halves,)),
            dma((halves,)),
            dma((halves,)),
            dma((halves,)),
            dma((halves,)),
            dma((halves,)),
            dma,
            dma,
        ],
        compiler_params=pltpu.CompilerParams(
            collective_id=0, has_side_effects=True, vmem_limit_bytes=32 * 1024 * 1024
        ),
        cost_estimate=pl.CostEstimate(flops=2 * 10**9, bytes_accessed=2 * 10**6, transcendentals=0),
    )(
        *[
            fixed(a)
            for a in (
                queries, keys, values, filters, short_weight, skip_gain[None, :], residual, norm_gain[None, :],
                jnp.asarray(matrices), jnp.asarray(twist),
            )
        ]
    )
    stream_out = total.astype(BF16)
    normed = (stream_out.astype(F32) * scale[0][:, None] * gain[0]).astype(BF16)
    return stream_out, normed


def solution(mesh):
    placed = (
        P("seq", "ch"),
        P("seq", "ch"),
        P("seq", "ch"),
        P("seq", "ch"),
        P(None, None, "ch"),
        P("ch"),
        P("seq", "ch"),
        P("ch"),
    )
    return jax.shard_map(
        shards,
        mesh=mesh,
        in_specs=placed,
        out_specs=(P("seq", "ch"), P("seq", "ch")),
        check_vma=False,
    )
```

```python
import functools
import math

import jax
import jax.numpy as jnp
import numpy as np
from jax import lax
from jax.experimental import pallas as pl
from jax.experimental.pallas import tpu as pltpu
from jax.sharding import PartitionSpec as P

F32 = jnp.float32
BF16 = jnp.bfloat16
LANES = 128
GROUP = 16
PARTS = 32
ROOT = math.sqrt(0.5)

KEPT = (
    [0, 8, 16, 24, 32]
    + [1 + 8 * b for b in range(8)]
    + [2 + 8 * b for b in range(8)]
    + [3 + 8 * b for b in range(8)]
    + [4 + 8 * b for b in range(4)]
)
PLACE = {k1: i for i, k1 in enumerate(KEPT)}
ROWS = len(KEPT) * GROUP
CHUNK = 11 * GROUP


STEPS = sorted(
    ((dx, dy, dc) for dx in range(4) for dy in range(4) for dc in range(2) if dx + dy + dc > 0),
    key=lambda step: -(min(step[0], 4 - step[0]) + min(step[1], 4 - step[1])),
)


ABS = sorted(range(32), key=lambda p: (p // 8 + p // 2 % 4, -(p % 2)))


def tables():
    lane = np.arange(LANES)
    angle = 2.0 * np.pi * (np.outer(lane, lane) % LANES) / LANES
    cos, sin = np.cos(angle), np.sin(angle)
    forward = np.block([[cos, -sin], [sin, cos]])
    backward = np.block([[cos, sin], [-sin, cos]])
    parts = []
    for matrix in (forward, backward):
        high = matrix.astype(np.float32).astype(jnp.bfloat16)
        low = (matrix - high.astype(np.float64)).astype(np.float32).astype(jnp.bfloat16)
        parts += [high, low]
    matrices = np.stack(parts)
    turn = 2.0 * np.pi * np.outer(KEPT, lane) / (64 * LANES)
    weight = np.where(np.isin(KEPT, [0, 32]), 1.0, 2.0)[:, None] / (64 * LANES)
    twist = np.stack([np.cos(turn), -np.sin(turn), weight * np.cos(turn), weight * np.sin(turn)])
    return matrices, twist.astype(np.float32)


def plus(a, b):
    if a is None:
        return b
    return a if b is None else a + b


def neg(a):
    return None if a is None else -a


def minus(a, b):
    if b is None:
        return a
    return -b if a is None else a - b


def scaled(a, factor):
    return None if a is None else a * factor


def cplus(a, b):
    return (plus(a[0], b[0]), plus(a[1], b[1]))


def cminus(a, b):
    return (minus(a[0], b[0]), minus(a[1], b[1]))


def quarter(a, sign):
    return (neg(a[1]), a[0]) if sign > 0 else (a[1], neg(a[0]))


def turned(a, angle):
    cos, sin = math.cos(angle), math.sin(angle)
    if angle == 0.0:
        return a
    return (
        minus(scaled(a[0], cos), scaled(a[1], sin)),
        plus(scaled(a[1], cos), scaled(a[0], sin)),
    )


def dft4(z, sign):
    a, b = cplus(z[0], z[2]), cminus(z[0], z[2])
    c, d = cplus(z[1], z[3]), quarter(cminus(z[1], z[3]), sign)
    return [cplus(a, c), cplus(b, d), cminus(a, c), cminus(b, d)]


def dft8(z, sign):
    even, odd = dft4(z[0::2], sign), dft4(z[1::2], sign)
    a, b = odd[1], odd[3]
    if sign > 0:
        first = (scaled(minus(a[0], a[1]), ROOT), scaled(plus(a[0], a[1]), ROOT))
        third = (scaled(plus(b[0], b[1]), -ROOT), scaled(minus(b[0], b[1]), ROOT))
    else:
        first = (scaled(plus(a[0], a[1]), ROOT), scaled(minus(a[1], a[0]), ROOT))
        third = (scaled(minus(b[1], b[0]), ROOT), scaled(plus(b[0], b[1]), -ROOT))
    odd = [odd[0], first, quarter(odd[2], sign), third]
    return [cplus(e, o) for e, o in zip(even, odd)] + [cminus(e, o) for e, o in zip(even, odd)]


def forward64(x):
    column = [[None] * 8 for _ in range(5)]
    for s in range(8):
        x0, x1, x2, x3 = x[s], x[8 + s], x[16 + s], x[24 + s]
        a, b, c, d = x0 + x2, x1 + x3, x0 - x2, (x1 - x3)
        rb, rd = b * ROOT, d * ROOT
        values = [(a + b, None), (x0 + rd, -x2 - rb), (c, -d), (x0 - rd, x2 - rb), (a - b, None)]
        for k in range(5):
            column[k][s] = turned(values[k], -2.0 * math.pi * s * k / 64)
    out = {}
    for k in range(5):
        result = dft8(column[k], -1)
        for b in range((5, 8, 8, 8, 4)[k]):
            out[k + 8 * b] = result[b]
    return out


def backward64(get):
    v = []
    for k in range(5):
        count = (5, 8, 8, 8, 4)[k]
        z = [get(k + 8 * b) if b < count else (None, None) for b in range(8)]
        if k == 0:
            z[0], z[4] = (z[0][0], None), (z[4][0], None)
        u = dft8(z, 1)
        v.append([turned(u[s], 2.0 * math.pi * s * k / 64) for s in range(8)])
    y = [None] * 32
    for s in range(8):
        (a, _), (br, bi), (cr, ci), (dr, di), (e, _) = [v[k][s] for k in range(5)]
        p, m = a + e, a - e
        y[s] = (p + cr) + (br + dr)
        y[16 + s] = (p - cr) + (di - bi)
        f, g = (br - dr) * ROOT, (bi + di) * ROOT
        y[8 + s] = (m - ci) + (f - g)
        y[24 + s] = (m + ci) - (f + g)
    return y


def split(a):
    high = a.astype(BF16)
    return high, (a - high.astype(F32)).astype(BF16)


def matmul(a, matrix):
    return jnp.dot(a, matrix, preferred_element_type=F32)


def product3(high, low, matrix_high, matrix_low):
    return matmul(high, matrix_high) + (matmul(low, matrix_high) + matmul(high, matrix_low))


def kernel(
    queries, keys, values, filters, short_taps, skip, residual, gain, matrices, twist,
    total_f, scale_v, gain_v,
    q_in, k_in, v_in, f_in, r_in, short_weight, skip_gain, mat, tw, tail_kv, halo, ext, mixed, short_q, base,
    send_f, send_m, got_f, got_m, send_y, got_y, a_high, a_low, spec_f, back, sums, own_sum,
    in_sem, halo_send, halo_recv, f_send, f_recv, m_send, m_recv, y_send, y_recv, p_send, p_recv,
):
    parts, rounds = lax.axis_size("seq"), lax.axis_size("ch")
    me, plane = lax.axis_index("seq"), lax.axis_index("ch")
    rows, width = q_in.shape
    own = width // parts
    halves = own // GROUP
    blocks = width // LANES

    barrier = pltpu.get_barrier_semaphore()

    x, y, core = me // 8, lax.rem(me // 2, 4), lax.rem(me, 2)
    peers = [
        lax.rem(x + dx, 4) * 8 + lax.rem(y + dy, 4) * 2 + lax.rem(core + dc, 2)
        for dx, dy, dc in STEPS
    ]
    for peer in peers:
        pl.semaphore_signal(barrier, inc=1, device_id={"seq": peer})

    @pl.loop(1, rounds)
    def _(d):
        pl.semaphore_signal(barrier, inc=1, device_id={"ch": lax.rem(plane + d, rounds)})

    loads = [
        pltpu.make_async_copy(source, target, in_sem.at[i])
        for i, (source, target) in enumerate(
            [
                (filters, f_in), (keys, k_in), (values, v_in), (queries, q_in), (residual, r_in),
                (short_taps, short_weight), (skip, skip_gain), (gain, gain_v),
                (matrices, mat), (twist, tw),
            ]
        )
    ]
    for load in loads:
        load.start()

    def lanes(b):
        return pl.ds(pl.multiple_of(b * LANES, LANES), LANES)

    loads[0].wait()

    @pl.loop(0, blocks)
    def _(b):
        send_f[lanes(b), :] = f_in[:, lanes(b)].T

    for i in (1, 2, 3):
        loads[i].wait()
    last = pl.ds(rows - GROUP, GROUP)
    tail_kv[...] = jnp.concatenate(
        [k_in[last, :].astype(F32)[8:], v_in[last, :].astype(F32)[8:]], axis=0
    ).astype(BF16)

    pl.semaphore_wait(barrier, parts - 1 + rounds - 1)

    after = {"seq": lax.rem(me + 1, parts)}
    tails = [
        pltpu.make_async_remote_copy(
            src_ref=source,
            dst_ref=halo.at[i],
            send_sem=halo_send.at[i],
            recv_sem=halo_recv.at[i],
            device_id=after,
        )
        for i, source in enumerate((tail_kv, q_in.at[pl.ds(rows - GROUP, GROUP), :]))
    ]
    tails[0].start()
    tails[1].start()

    def own_rows(peer, h):
        return pl.ds(pl.multiple_of(h * (width // halves) + peer * GROUP, GROUP), GROUP)

    def exchange_abs(source, target, send_sem, recv_sem):
        pltpu.make_async_copy(source(me), target, recv_sem).start()
        for peer in ABS:
            @pl.when(me != peer)
            def _():
                pltpu.make_async_remote_copy(
                    src_ref=source(peer),
                    dst_ref=target,
                    send_sem=send_sem,
                    recv_sem=recv_sem,
                    device_id={"seq": peer},
                ).start()

    def exchange(source, target, send_sem, recv_sem):
        pltpu.make_async_copy(source(me), target, recv_sem).start()
        for peer in peers:
            pltpu.make_async_remote_copy(
                src_ref=source(peer),
                dst_ref=target,
                send_sem=send_sem,
                recv_sem=recv_sem,
                device_id={"seq": peer},
            ).start()

    for h in range(halves):
        exchange(
            lambda peer: send_f.at[own_rows(peer, h)], got_f.at[h, me], f_send.at[h], f_recv.at[h]
        )

    for i, stream in enumerate((q_in, k_in, v_in)):
        ext[i, pl.ds(8, rows), :] = stream[...].astype(F32)

    def short(i, b, count):
        weights = short_weight[i, :, lanes(b)].astype(F32)
        total = weights[0:1] * ext[i, pl.ds(8, count), lanes(b)]
        for j in range(1, weights.shape[0]):
            total = total + weights[j : j + 1] * ext[i, pl.ds(8 - j, count), lanes(b)]
        return total

    loads[5].wait()
    for i in range(3):
        ext[i, pl.ds(0, 8), :] = jnp.zeros((8, width), F32)

    @pl.loop(0, blocks)
    def _(b):
        product = short(1, b, rows) * short(2, b, rows)
        mixed[:, lanes(b)] = product.astype(BF16)
        send_m[lanes(b), :] = product.astype(BF16).T

    tails[0].wait_recv()
    first = me == 0
    head = jnp.where(first, 0.0, halo[0].astype(F32))
    ext[1, pl.ds(0, 8), :] = head[:8]
    ext[2, pl.ds(0, 8), :] = head[8:]

    for h in range(halves):

        @pl.loop(h * blocks // halves, (h + 1) * blocks // halves)
        def _(b):
            product = short(1, b, GROUP) * short(2, b, GROUP)
            mixed[pl.ds(0, GROUP), lanes(b)] = product.astype(BF16)
            send_m[lanes(b), pl.ds(0, GROUP)] = product.astype(BF16).T

        exchange(
            lambda peer: send_m.at[own_rows(peer, h)], got_m.at[h, me], m_send.at[h], m_recv.at[h]
        )

    loads[8].wait()
    loads[9].wait()

    def twisted(value, i, which):
        cos, sin = tw[which, pl.ds(i, 1), :], tw[which + 1, pl.ds(i, 1), :]
        if value[1] is None:
            return value[0] * cos, value[0] * sin
        return value[0] * cos - value[1] * sin, value[1] * cos + value[0] * sin

    def first_stage(got, h):
        spectrum = forward64([got[h, s].astype(F32) for s in range(PARTS)])
        for k1 in KEPT:
            i = PLACE[k1]
            for half, part in enumerate(twisted(spectrum[k1], i, 0)):
                place = (pl.ds(i * GROUP, GROUP), pl.ds(half * LANES, LANES))
                a_high[place], a_low[place] = split(part)

    @pl.loop(0, halves)
    def _(h):
        pltpu.make_async_copy(got_f.at[h], got_f.at[h], f_recv.at[h]).wait()
        first_stage(got_f, h)
        for c in range(ROWS // CHUNK):
            chunk = pl.ds(c * CHUNK, CHUNK)
            spec_f[h, chunk, :] = product3(a_high[chunk, :], a_low[chunk, :], mat[0], mat[1])

    @pl.loop(0, halves)
    def _(h):
        pass
        pltpu.make_async_copy(got_m.at[h], got_m.at[h], m_recv.at[h]).wait()
        first_stage(got_m, h)
        for c in range(ROWS // CHUNK):
            chunk = pl.ds(c * CHUNK, CHUNK)
            signal = product3(a_high[chunk, :], a_low[chunk, :], mat[0], mat[1])
            taps = spec_f[h, chunk, :]
            sr, si = signal[:, :LANES], signal[:, LANES:]
            fr, fi = taps[:, :LANES], taps[:, LANES:]
            both = jnp.concatenate([sr * fr - si * fi, sr * fi + si * fr], axis=1)
            back[chunk, :] = product3(*split(both), mat[2], mat[3])

        def value(k1):
            i = PLACE[k1]
            part = pl.ds(i * GROUP, GROUP)
            return twisted((back[part, pl.ds(0, LANES)], back[part, pl.ds(LANES, LANES)]), i, 2)

        for s, y in enumerate(backward64(value)):
            send_y[h, s] = y.astype(BF16)
        exchange_abs(lambda peer: send_y.at[h, peer], got_y.at[own_rows(me, h)], y_send.at[h], y_recv.at[h])

    tails[1].wait_recv()
    ext[0, pl.ds(0, 8), :] = jnp.where(first, 0.0, halo[1].astype(F32))[8:]
    loads[4].wait()
    loads[6].wait()

    @pl.loop(0, blocks)
    def _(b):
        gate = short(0, b, rows)
        short_q[:, lanes(b)] = gate
        direct = skip_gain[:, lanes(b)] * mixed[:, lanes(b)].astype(F32)
        base[:, lanes(b)] = r_in[:, lanes(b)].astype(F32) + gate * direct

    partial = jnp.zeros((rows, LANES), F32)
    for h in range(halves):
        arrived = got_y.at[pl.ds(h * (width // halves), width // halves)]
        pltpu.make_async_copy(arrived, arrived, y_recv.at[h]).wait()
        for b in range(h * blocks // halves, (h + 1) * blocks // halves):
            at = pl.ds(b * LANES, LANES)
            conv = got_y[at, :].T.astype(F32)
            value = (base[:, at] + short_q[:, at] * conv).astype(BF16).astype(F32)
            total_f[:, at] = value
            partial = partial + value * value

    own_sum[...] = jnp.sum(partial.T, axis=0, keepdims=True)
    pltpu.make_async_copy(own_sum, sums.at[plane], p_recv).start()

    for d in sorted(range(1, rounds), key=lambda d: -min(d, rounds - d)):
        pltpu.make_async_remote_copy(
            src_ref=own_sum,
            dst_ref=sums.at[plane],
            send_sem=p_send,
            recv_sem=p_recv,
            device_id={"ch": lax.rem(plane + d, rounds)},
        ).start()

    for copy in tails:
        copy.wait_send()
    others = pl.ds(0, parts - 1)
    for h in range(halves):
        pass
        pltpu.make_async_copy(got_f.at[h, others], got_f.at[h, others], f_send.at[h]).wait()
        pltpu.make_async_copy(got_m.at[h, others], got_m.at[h, others], m_send.at[h]).wait()
        pltpu.make_async_copy(got_m.at[h, others], got_m.at[h, others], y_send.at[h]).wait()
    if rounds > 1:
        most = sums.at[pl.ds(0, rounds - 1)]
        pltpu.make_async_copy(most, most, p_send).wait()
    loads[7].wait()

    pltpu.make_async_copy(sums, sums, p_recv).wait()
    power = jnp.sum(sums[...], axis=0) / (width * rounds)
    scale_v[...] = lax.rsqrt(power + 1e-05)


def shards(queries, keys, values, filters, short_weight, skip_gain, residual, norm_gain):
    rows, width = queries.shape
    parts, rounds = lax.axis_size("seq"), lax.axis_size("ch")
    taps = short_weight.shape[1]
    own = width // parts
    halves = own // GROUP
    assert parts == PARTS and rows == LANES and own % GROUP == 0
    matrices, twist = tables()
    block = (rows, width)
    whole = pl.BlockSpec(memory_space=pltpu.HBM)
    near = pl.BlockSpec(memory_space=pltpu.VMEM)
    dma = pltpu.SemaphoreType.DMA
    fixed = lambda a: pltpu.with_memory_space_constraint(a, pltpu.HBM)
    total, scale, gain = pl.pallas_call(
        kernel,
        out_shape=(jax.ShapeDtypeStruct(block, F32), jax.ShapeDtypeStruct((1, rows), F32), jax.ShapeDtypeStruct((1, width), F32)),
        in_specs=[whole] * 10,
        out_specs=(near, near, near),
        scratch_shapes=[
            pltpu.VMEM(block, BF16),
            pltpu.VMEM(block, BF16),
            pltpu.VMEM(block, BF16),
            pltpu.VMEM(block, BF16),
            pltpu.VMEM(block, BF16),
            pltpu.VMEM((3, taps, width), BF16),
            pltpu.VMEM((1, width), F32),
            pltpu.VMEM(matrices.shape, BF16),
            pltpu.VMEM(twist.shape, F32),
            pltpu.VMEM((GROUP, width), BF16),
            pltpu.VMEM((2, GROUP, width), BF16),
            pltpu.VMEM((3, rows + 8, width), F32),
            pltpu.VMEM(block, BF16),
            pltpu.VMEM(block, F32),
            pltpu.VMEM(block, F32),
            pltpu.VMEM((width, rows), BF16),
            pltpu.VMEM((width, rows), BF16),
            pltpu.VMEM((halves, parts, GROUP, LANES), BF16),
            pltpu.VMEM((halves, parts, GROUP, LANES), BF16),
            pltpu.VMEM((halves, parts, GROUP, LANES), BF16),
            pltpu.VMEM((width, rows), BF16),
            pltpu.VMEM((ROWS, 2 * LANES), BF16),
            pltpu.VMEM((ROWS, 2 * LANES), BF16),
            pltpu.VMEM((halves, ROWS, 2 * LANES), F32),
            pltpu.VMEM((ROWS, 2 * LANES), F32),
            pltpu.VMEM((rounds, 1, LANES), F32),
            pltpu.VMEM((1, LANES), F32),
            dma((10,)),
            dma((2,)),
            dma((2,)),
            dma((halves,)),
            dma((halves,)),
            dma((halves,)),
            dma((halves,)),
            dma((halves,)),
            dma((halves,)),
            dma,
            dma,
        ],
        compiler_params=pltpu.CompilerParams(
            collective_id=0, has_side_effects=True, vmem_limit_bytes=32 * 1024 * 1024
        ),
        cost_estimate=pl.CostEstimate(flops=2 * 10**9, bytes_accessed=2 * 10**6, transcendentals=0),
    )(
        *[
            fixed(a)
            for a in (
                queries, keys, values, filters, short_weight, skip_gain[None, :], residual, norm_gain[None, :],
                jnp.asarray(matrices), jnp.asarray(twist),
            )
        ]
    )
    stream_out = total.astype(BF16)
    normed = (stream_out.astype(F32) * scale[0][:, None] * gain[0]).astype(BF16)
    return stream_out, normed


def solution(mesh):
    placed = (
        P("seq", "ch"),
        P("seq", "ch"),
        P("seq", "ch"),
        P("seq", "ch"),
        P(None, None, "ch"),
        P("ch"),
        P("seq", "ch"),
        P("ch"),
    )
    return jax.shard_map(
        shards,
        mesh=mesh,
        in_specs=placed,
        out_specs=(P("seq", "ch"), P("seq", "ch")),
        check_vma=False,
    )
```

```python
import functools
import math

import jax
import jax.numpy as jnp
import numpy as np
from jax import lax
from jax.experimental import pallas as pl
from jax.experimental.pallas import tpu as pltpu
from jax.sharding import PartitionSpec as P

F32 = jnp.float32
BF16 = jnp.bfloat16
LANES = 128
GROUP = 16
PARTS = 32
ROOT = math.sqrt(0.5)

KEPT = (
    [0, 8, 16, 24, 32]
    + [1 + 8 * b for b in range(8)]
    + [2 + 8 * b for b in range(8)]
    + [3 + 8 * b for b in range(8)]
    + [4 + 8 * b for b in range(4)]
)
PLACE = {k1: i for i, k1 in enumerate(KEPT)}
ROWS = len(KEPT) * GROUP
CHUNK = 11 * GROUP


STEPS = sorted(
    ((dx, dy, dc) for dx in range(4) for dy in range(4) for dc in range(2) if dx + dy + dc > 0),
    key=lambda step: -(min(step[0], 4 - step[0]) + min(step[1], 4 - step[1])),
)


ABS = sorted(range(32), key=lambda p: (p // 8 + p // 2 % 4, -(p % 2)))


def tables():
    lane = np.arange(LANES)
    angle = 2.0 * np.pi * (np.outer(lane, lane) % LANES) / LANES
    cos, sin = np.cos(angle), np.sin(angle)
    forward = np.block([[cos, -sin], [sin, cos]])
    backward = np.block([[cos, sin], [-sin, cos]])
    parts = []
    for matrix in (forward, backward):
        high = matrix.astype(np.float32).astype(jnp.bfloat16)
        low = (matrix - high.astype(np.float64)).astype(np.float32).astype(jnp.bfloat16)
        parts += [high, low]
    matrices = np.stack(parts)
    turn = 2.0 * np.pi * np.outer(KEPT, lane) / (64 * LANES)
    weight = np.where(np.isin(KEPT, [0, 32]), 1.0, 2.0)[:, None] / (64 * LANES)
    twist = np.stack([np.cos(turn), -np.sin(turn), weight * np.cos(turn), weight * np.sin(turn)])
    return matrices, twist.astype(np.float32)


def plus(a, b):
    if a is None:
        return b
    return a if b is None else a + b


def neg(a):
    return None if a is None else -a


def minus(a, b):
    if b is None:
        return a
    return -b if a is None else a - b


def scaled(a, factor):
    return None if a is None else a * factor


def cplus(a, b):
    return (plus(a[0], b[0]), plus(a[1], b[1]))


def cminus(a, b):
    return (minus(a[0], b[0]), minus(a[1], b[1]))


def quarter(a, sign):
    return (neg(a[1]), a[0]) if sign > 0 else (a[1], neg(a[0]))


def turned(a, angle):
    cos, sin = math.cos(angle), math.sin(angle)
    if angle == 0.0:
        return a
    return (
        minus(scaled(a[0], cos), scaled(a[1], sin)),
        plus(scaled(a[1], cos), scaled(a[0], sin)),
    )


def dft4(z, sign):
    a, b = cplus(z[0], z[2]), cminus(z[0], z[2])
    c, d = cplus(z[1], z[3]), quarter(cminus(z[1], z[3]), sign)
    return [cplus(a, c), cplus(b, d), cminus(a, c), cminus(b, d)]


def dft8(z, sign):
    even, odd = dft4(z[0::2], sign), dft4(z[1::2], sign)
    a, b = odd[1], odd[3]
    if sign > 0:
        first = (scaled(minus(a[0], a[1]), ROOT), scaled(plus(a[0], a[1]), ROOT))
        third = (scaled(plus(b[0], b[1]), -ROOT), scaled(minus(b[0], b[1]), ROOT))
    else:
        first = (scaled(plus(a[0], a[1]), ROOT), scaled(minus(a[1], a[0]), ROOT))
        third = (scaled(minus(b[1], b[0]), ROOT), scaled(plus(b[0], b[1]), -ROOT))
    odd = [odd[0], first, quarter(odd[2], sign), third]
    return [cplus(e, o) for e, o in zip(even, odd)] + [cminus(e, o) for e, o in zip(even, odd)]


def forward64(x):
    column = [[None] * 8 for _ in range(5)]
    for s in range(8):
        x0, x1, x2, x3 = x[s], x[8 + s], x[16 + s], x[24 + s]
        a, b, c, d = x0 + x2, x1 + x3, x0 - x2, (x1 - x3)
        rb, rd = b * ROOT, d * ROOT
        values = [(a + b, None), (x0 + rd, -x2 - rb), (c, -d), (x0 - rd, x2 - rb), (a - b, None)]
        for k in range(5):
            column[k][s] = turned(values[k], -2.0 * math.pi * s * k / 64)
    out = {}
    for k in range(5):
        result = dft8(column[k], -1)
        for b in range((5, 8, 8, 8, 4)[k]):
            out[k + 8 * b] = result[b]
    return out


def backward64(get):
    v = []
    for k in range(5):
        count = (5, 8, 8, 8, 4)[k]
        z = [get(k + 8 * b) if b < count else (None, None) for b in range(8)]
        if k == 0:
            z[0], z[4] = (z[0][0], None), (z[4][0], None)
        u = dft8(z, 1)
        v.append([turned(u[s], 2.0 * math.pi * s * k / 64) for s in range(8)])
    y = [None] * 32
    for s in range(8):
        (a, _), (br, bi), (cr, ci), (dr, di), (e, _) = [v[k][s] for k in range(5)]
        p, m = a + e, a - e
        y[s] = (p + cr) + (br + dr)
        y[16 + s] = (p - cr) + (di - bi)
        f, g = (br - dr) * ROOT, (bi + di) * ROOT
        y[8 + s] = (m - ci) + (f - g)
        y[24 + s] = (m + ci) - (f + g)
    return y


def split(a):
    high = a.astype(BF16)
    return high, (a - high.astype(F32)).astype(BF16)


def matmul(a, matrix):
    return jnp.dot(a, matrix, preferred_element_type=F32)


def product3(high, low, matrix_high, matrix_low):
    return matmul(high, matrix_high) + (matmul(low, matrix_high) + matmul(high, matrix_low))


def kernel(
    queries, keys, values, filters, short_taps, skip, residual, gain, matrices, twist,
    total_f, scale_v, gain_v,
    q_in, k_in, v_in, f_in, r_in, short_weight, skip_gain, mat, tw, tail_kv, halo, ext, mixed, short_q, base,
    send_f, send_m, got_f, got_m, send_y, got_y, a_high, a_low, spec_f, back, sums, own_sum,
    in_sem, halo_send, halo_recv, f_send, f_recv, m_send, m_recv, y_send, y_recv, p_send, p_recv,
):
    parts, rounds = lax.axis_size("seq"), lax.axis_size("ch")
    me, plane = lax.axis_index("seq"), lax.axis_index("ch")
    rows, width = q_in.shape
    own = width // parts
    halves = own // GROUP
    blocks = width // LANES

    barrier = pltpu.get_barrier_semaphore()

    x, y, core = me // 8, lax.rem(me // 2, 4), lax.rem(me, 2)
    peers = [
        lax.rem(x + dx, 4) * 8 + lax.rem(y + dy, 4) * 2 + lax.rem(core + dc, 2)
        for dx, dy, dc in STEPS
    ]
    for peer in peers:
        pl.semaphore_signal(barrier, inc=1, device_id={"seq": peer})

    @pl.loop(1, rounds)
    def _(d):
        pl.semaphore_signal(barrier, inc=1, device_id={"ch": lax.rem(plane + d, rounds)})

    loads = [
        pltpu.make_async_copy(source, target, in_sem.at[i])
        for i, (source, target) in enumerate(
            [
                (filters, f_in), (keys, k_in), (values, v_in), (queries, q_in), (residual, r_in),
                (short_taps, short_weight), (skip, skip_gain), (gain, gain_v),
                (matrices, mat), (twist, tw),
            ]
        )
    ]
    for load in loads:
        load.start()

    def lanes(b):
        return pl.ds(pl.multiple_of(b * LANES, LANES), LANES)

    loads[0].wait()

    @pl.loop(0, blocks)
    def _(b):
        send_f[lanes(b), :] = f_in[:, lanes(b)].T

    for i in (1, 2, 3):
        loads[i].wait()
    last = pl.ds(rows - GROUP, GROUP)
    tail_kv[...] = jnp.concatenate(
        [k_in[last, :].astype(F32)[8:], v_in[last, :].astype(F32)[8:]], axis=0
    ).astype(BF16)

    pl.semaphore_wait(barrier, parts - 1 + rounds - 1)

    after = {"seq": lax.rem(me + 1, parts)}
    tails = [
        pltpu.make_async_remote_copy(
            src_ref=source,
            dst_ref=halo.at[i],
            send_sem=halo_send.at[i],
            recv_sem=halo_recv.at[i],
            device_id=after,
        )
        for i, source in enumerate((tail_kv, q_in.at[pl.ds(rows - GROUP, GROUP), :]))
    ]
    tails[0].start()
    tails[1].start()

    def own_rows(peer, h):
        return pl.ds(pl.multiple_of(h * (width // halves) + peer * GROUP, GROUP), GROUP)

    def exchange_abs(source, target, send_sem, recv_sem):
        pltpu.make_async_copy(source(me), target, recv_sem).start()
        for peer in ABS:
            @pl.when(me != peer)
            def _():
                pltpu.make_async_remote_copy(
                    src_ref=source(peer),
                    dst_ref=target,
                    send_sem=send_sem,
                    recv_sem=recv_sem,
                    device_id={"seq": peer},
                ).start()

    def exchange(source, target, send_sem, recv_sem):
        pltpu.make_async_copy(source(me), target, recv_sem).start()
        for peer in peers:
            pltpu.make_async_remote_copy(
                src_ref=source(peer),
                dst_ref=target,
                send_sem=send_sem,
                recv_sem=recv_sem,
                device_id={"seq": peer},
            ).start()

    for h in range(halves):
        exchange(
            lambda peer: send_f.at[own_rows(peer, h)], got_f.at[h, me], f_send.at[h], f_recv.at[h]
        )

    for i, stream in enumerate((q_in, k_in, v_in)):
        ext[i, pl.ds(8, rows), :] = stream[...].astype(F32)

    def short(i, b, count):
        weights = short_weight[i, :, lanes(b)].astype(F32)
        total = weights[0:1] * ext[i, pl.ds(8, count), lanes(b)]
        for j in range(1, weights.shape[0]):
            total = total + weights[j : j + 1] * ext[i, pl.ds(8 - j, count), lanes(b)]
        return total

    loads[5].wait()
    for i in range(3):
        ext[i, pl.ds(0, 8), :] = jnp.zeros((8, width), F32)

    @pl.loop(0, blocks)
    def _(b):
        product = short(1, b, rows) * short(2, b, rows)
        mixed[:, lanes(b)] = product.astype(BF16)
        send_m[lanes(b), :] = product.astype(BF16).T

    tails[0].wait_recv()
    first = me == 0
    head = jnp.where(first, 0.0, halo[0].astype(F32))
    ext[1, pl.ds(0, 8), :] = head[:8]
    ext[2, pl.ds(0, 8), :] = head[8:]

    for h in range(halves):

        @pl.loop(h * blocks // halves, (h + 1) * blocks // halves)
        def _(b):
            product = short(1, b, GROUP) * short(2, b, GROUP)
            mixed[pl.ds(0, GROUP), lanes(b)] = product.astype(BF16)
            send_m[lanes(b), pl.ds(0, GROUP)] = product.astype(BF16).T

        exchange(
            lambda peer: send_m.at[own_rows(peer, h)], got_m.at[h, me], m_send.at[h], m_recv.at[h]
        )

    loads[8].wait()
    loads[9].wait()

    def twisted(value, i, which):
        cos, sin = tw[which, pl.ds(i, 1), :], tw[which + 1, pl.ds(i, 1), :]
        if value[1] is None:
            return value[0] * cos, value[0] * sin
        return value[0] * cos - value[1] * sin, value[1] * cos + value[0] * sin

    def first_stage(got, h):
        spectrum = forward64([got[h, s].astype(F32) for s in range(PARTS)])
        for k1 in KEPT:
            i = PLACE[k1]
            for half, part in enumerate(twisted(spectrum[k1], i, 0)):
                place = (h, pl.ds(i * GROUP, GROUP), pl.ds(half * LANES, LANES))
                a_high[place], a_low[place] = split(part)

    @pl.loop(0, halves)
    def _(h):
        pltpu.make_async_copy(got_f.at[h], got_f.at[h], f_recv.at[h]).wait()
        first_stage(got_f, h)
        for c in range(ROWS // CHUNK):
            chunk = pl.ds(c * CHUNK, CHUNK)
            spec_f[h, chunk, :] = product3(a_high[h, chunk, :], a_low[h, chunk, :], mat[0], mat[1])

    def middle(h):
        for c in range(ROWS // CHUNK):
            chunk = pl.ds(c * CHUNK, CHUNK)
            signal = product3(a_high[h, chunk, :], a_low[h, chunk, :], mat[0], mat[1])
            taps = spec_f[h, chunk, :]
            sr, si = signal[:, :LANES], signal[:, LANES:]
            fr, fi = taps[:, :LANES], taps[:, LANES:]
            both = jnp.concatenate([sr * fr - si * fi, sr * fi + si * fr], axis=1)
            back[h, chunk, :] = product3(*split(both), mat[2], mat[3])

    def last_stage(h):
        def value(k1):
            i = PLACE[k1]
            part = pl.ds(i * GROUP, GROUP)
            return twisted(
                (back[h, part, pl.ds(0, LANES)], back[h, part, pl.ds(LANES, LANES)]), i, 2
            )

        for s, y in enumerate(backward64(value)):
            send_y[h, s] = y.astype(BF16)

    for step in range(halves + 2):
        if step < halves:
            pltpu.make_async_copy(got_m.at[step], got_m.at[step], m_recv.at[step]).wait()
            first_stage(got_m, step)
        if 1 <= step <= halves:
            middle(step - 1)
        if step >= 2:
            h = step - 2
            last_stage(h)
            exchange_abs(
                lambda peer: send_y.at[h, peer], got_y.at[own_rows(me, h)], y_send.at[h], y_recv.at[h]
            )

    tails[1].wait_recv()
    ext[0, pl.ds(0, 8), :] = jnp.where(first, 0.0, halo[1].astype(F32))[8:]
    loads[4].wait()
    loads[6].wait()

    @pl.loop(0, blocks)
    def _(b):
        gate = short(0, b, rows)
        short_q[:, lanes(b)] = gate
        direct = skip_gain[:, lanes(b)] * mixed[:, lanes(b)].astype(F32)
        base[:, lanes(b)] = r_in[:, lanes(b)].astype(F32) + gate * direct

    partial = jnp.zeros((rows, LANES), F32)
    for h in range(halves):
        arrived = got_y.at[pl.ds(h * (width // halves), width // halves)]
        pltpu.make_async_copy(arrived, arrived, y_recv.at[h]).wait()
        for b in range(h * blocks // halves, (h + 1) * blocks // halves):
            at = pl.ds(b * LANES, LANES)
            conv = got_y[at, :].T.astype(F32)
            value = (base[:, at] + short_q[:, at] * conv).astype(BF16).astype(F32)
            total_f[:, at] = value
            partial = partial + value * value

    own_sum[...] = jnp.sum(partial.T, axis=0, keepdims=True)
    pltpu.make_async_copy(own_sum, sums.at[plane], p_recv).start()

    for d in sorted(range(1, rounds), key=lambda d: -min(d, rounds - d)):
        pltpu.make_async_remote_copy(
            src_ref=own_sum,
            dst_ref=sums.at[plane],
            send_sem=p_send,
            recv_sem=p_recv,
            device_id={"ch": lax.rem(plane + d, rounds)},
        ).start()

    for copy in tails:
        copy.wait_send()
    others = pl.ds(0, parts - 1)
    for h in range(halves):
        pass
        pltpu.make_async_copy(got_f.at[h, others], got_f.at[h, others], f_send.at[h]).wait()
        pltpu.make_async_copy(got_m.at[h, others], got_m.at[h, others], m_send.at[h]).wait()
        pltpu.make_async_copy(got_m.at[h, others], got_m.at[h, others], y_send.at[h]).wait()
    if rounds > 1:
        most = sums.at[pl.ds(0, rounds - 1)]
        pltpu.make_async_copy(most, most, p_send).wait()
    loads[7].wait()

    pltpu.make_async_copy(sums, sums, p_recv).wait()
    power = jnp.sum(sums[...], axis=0) / (width * rounds)
    scale_v[...] = lax.rsqrt(power + 1e-05)


def shards(queries, keys, values, filters, short_weight, skip_gain, residual, norm_gain):
    rows, width = queries.shape
    parts, rounds = lax.axis_size("seq"), lax.axis_size("ch")
    taps = short_weight.shape[1]
    own = width // parts
    halves = own // GROUP
    assert parts == PARTS and rows == LANES and own % GROUP == 0
    matrices, twist = tables()
    block = (rows, width)
    whole = pl.BlockSpec(memory_space=pltpu.HBM)
    near = pl.BlockSpec(memory_space=pltpu.VMEM)
    dma = pltpu.SemaphoreType.DMA
    fixed = lambda a: pltpu.with_memory_space_constraint(a, pltpu.HBM)
    total, scale, gain = pl.pallas_call(
        kernel,
        out_shape=(jax.ShapeDtypeStruct(block, F32), jax.ShapeDtypeStruct((1, rows), F32), jax.ShapeDtypeStruct((1, width), F32)),
        in_specs=[whole] * 10,
        out_specs=(near, near, near),
        scratch_shapes=[
            pltpu.VMEM(block, BF16),
            pltpu.VMEM(block, BF16),
            pltpu.VMEM(block, BF16),
            pltpu.VMEM(block, BF16),
            pltpu.VMEM(block, BF16),
            pltpu.VMEM((3, taps, width), BF16),
            pltpu.VMEM((1, width), F32),
            pltpu.VMEM(matrices.shape, BF16),
            pltpu.VMEM(twist.shape, F32),
            pltpu.VMEM((GROUP, width), BF16),
            pltpu.VMEM((2, GROUP, width), BF16),
            pltpu.VMEM((3, rows + 8, width), F32),
            pltpu.VMEM(block, BF16),
            pltpu.VMEM(block, F32),
            pltpu.VMEM(block, F32),
            pltpu.VMEM((width, rows), BF16),
            pltpu.VMEM((width, rows), BF16),
            pltpu.VMEM((halves, parts, GROUP, LANES), BF16),
            pltpu.VMEM((halves, parts, GROUP, LANES), BF16),
            pltpu.VMEM((halves, parts, GROUP, LANES), BF16),
            pltpu.VMEM((width, rows), BF16),
            pltpu.VMEM((halves, ROWS, 2 * LANES), BF16),
            pltpu.VMEM((halves, ROWS, 2 * LANES), BF16),
            pltpu.VMEM((halves, ROWS, 2 * LANES), F32),
            pltpu.VMEM((halves, ROWS, 2 * LANES), F32),
            pltpu.VMEM((rounds, 1, LANES), F32),
            pltpu.VMEM((1, LANES), F32),
            dma((10,)),
            dma((2,)),
            dma((2,)),
            dma((halves,)),
            dma((halves,)),
            dma((halves,)),
            dma((halves,)),
            dma((halves,)),
            dma((halves,)),
            dma,
            dma,
        ],
        compiler_params=pltpu.CompilerParams(
            collective_id=0, has_side_effects=True, vmem_limit_bytes=32 * 1024 * 1024
        ),
        cost_estimate=pl.CostEstimate(flops=2 * 10**9, bytes_accessed=2 * 10**6, transcendentals=0),
    )(
        *[
            fixed(a)
            for a in (
                queries, keys, values, filters, short_weight, skip_gain[None, :], residual, norm_gain[None, :],
                jnp.asarray(matrices), jnp.asarray(twist),
            )
        ]
    )
    stream_out = total.astype(BF16)
    normed = (stream_out.astype(F32) * scale[0][:, None] * gain[0]).astype(BF16)
    return stream_out, normed


def solution(mesh):
    placed = (
        P("seq", "ch"),
        P("seq", "ch"),
        P("seq", "ch"),
        P("seq", "ch"),
        P(None, None, "ch"),
        P("ch"),
        P("seq", "ch"),
        P("ch"),
    )
    return jax.shard_map(
        shards,
        mesh=mesh,
        in_specs=placed,
        out_specs=(P("seq", "ch"), P("seq", "ch")),
        check_vma=False,
    )
```

```python
import functools
import math

import jax
import jax.numpy as jnp
import numpy as np
from jax import lax
from jax.experimental import pallas as pl
from jax.experimental.pallas import tpu as pltpu
from jax.sharding import PartitionSpec as P

F32 = jnp.float32
BF16 = jnp.bfloat16
LANES = 128
GROUP = 16
PARTS = 32
ROOT = math.sqrt(0.5)

KEPT = (
    [0, 8, 16, 24, 32]
    + [1 + 8 * b for b in range(8)]
    + [2 + 8 * b for b in range(8)]
    + [3 + 8 * b for b in range(8)]
    + [4 + 8 * b for b in range(4)]
)
PLACE = {k1: i for i, k1 in enumerate(KEPT)}
ROWS = len(KEPT) * GROUP
CHUNK = 11 * GROUP


STEPS = sorted(
    ((dx, dy, dc) for dx in range(4) for dy in range(4) for dc in range(2) if dx + dy + dc > 0),
    key=lambda step: -(min(step[0], 4 - step[0]) + min(step[1], 4 - step[1])),
)


ABS = sorted(range(32), key=lambda p: (p // 8 + p // 2 % 4, -(p % 2)))


def tables():
    lane = np.arange(LANES)
    angle = 2.0 * np.pi * (np.outer(lane, lane) % LANES) / LANES
    cos, sin = np.cos(angle), np.sin(angle)
    forward = np.block([[cos, -sin], [sin, cos]])
    backward = np.block([[cos, sin], [-sin, cos]])
    parts = []
    for matrix in (forward, backward):
        high = matrix.astype(np.float32).astype(jnp.bfloat16)
        low = (matrix - high.astype(np.float64)).astype(np.float32).astype(jnp.bfloat16)
        parts += [high, low]
    matrices = np.stack(parts)
    turn = 2.0 * np.pi * np.outer(KEPT, lane) / (64 * LANES)
    weight = np.where(np.isin(KEPT, [0, 32]), 1.0, 2.0)[:, None] / (64 * LANES)
    twist = np.stack([np.cos(turn), -np.sin(turn), weight * np.cos(turn), weight * np.sin(turn)])
    return matrices, twist.astype(np.float32)


def plus(a, b):
    if a is None:
        return b
    return a if b is None else a + b


def neg(a):
    return None if a is None else -a


def minus(a, b):
    if b is None:
        return a
    return -b if a is None else a - b


def scaled(a, factor):
    return None if a is None else a * factor


def cplus(a, b):
    return (plus(a[0], b[0]), plus(a[1], b[1]))


def cminus(a, b):
    return (minus(a[0], b[0]), minus(a[1], b[1]))


def quarter(a, sign):
    return (neg(a[1]), a[0]) if sign > 0 else (a[1], neg(a[0]))


def turned(a, angle):
    cos, sin = math.cos(angle), math.sin(angle)
    if angle == 0.0:
        return a
    return (
        minus(scaled(a[0], cos), scaled(a[1], sin)),
        plus(scaled(a[1], cos), scaled(a[0], sin)),
    )


def dft4(z, sign):
    a, b = cplus(z[0], z[2]), cminus(z[0], z[2])
    c, d = cplus(z[1], z[3]), quarter(cminus(z[1], z[3]), sign)
    return [cplus(a, c), cplus(b, d), cminus(a, c), cminus(b, d)]


def dft8(z, sign):
    even, odd = dft4(z[0::2], sign), dft4(z[1::2], sign)
    a, b = odd[1], odd[3]
    if sign > 0:
        first = (scaled(minus(a[0], a[1]), ROOT), scaled(plus(a[0], a[1]), ROOT))
        third = (scaled(plus(b[0], b[1]), -ROOT), scaled(minus(b[0], b[1]), ROOT))
    else:
        first = (scaled(plus(a[0], a[1]), ROOT), scaled(minus(a[1], a[0]), ROOT))
        third = (scaled(minus(b[1], b[0]), ROOT), scaled(plus(b[0], b[1]), -ROOT))
    odd = [odd[0], first, quarter(odd[2], sign), third]
    return [cplus(e, o) for e, o in zip(even, odd)] + [cminus(e, o) for e, o in zip(even, odd)]


def forward64(x):
    column = [[None] * 8 for _ in range(5)]
    for s in range(8):
        x0, x1, x2, x3 = x[s], x[8 + s], x[16 + s], x[24 + s]
        a, b, c, d = x0 + x2, x1 + x3, x0 - x2, (x1 - x3)
        rb, rd = b * ROOT, d * ROOT
        values = [(a + b, None), (x0 + rd, -x2 - rb), (c, -d), (x0 - rd, x2 - rb), (a - b, None)]
        for k in range(5):
            column[k][s] = turned(values[k], -2.0 * math.pi * s * k / 64)
    out = {}
    for k in range(5):
        result = dft8(column[k], -1)
        for b in range((5, 8, 8, 8, 4)[k]):
            out[k + 8 * b] = result[b]
    return out


def backward64(get):
    v = []
    for k in range(5):
        count = (5, 8, 8, 8, 4)[k]
        z = [get(k + 8 * b) if b < count else (None, None) for b in range(8)]
        if k == 0:
            z[0], z[4] = (z[0][0], None), (z[4][0], None)
        u = dft8(z, 1)
        v.append([turned(u[s], 2.0 * math.pi * s * k / 64) for s in range(8)])
    y = [None] * 32
    for s in range(8):
        (a, _), (br, bi), (cr, ci), (dr, di), (e, _) = [v[k][s] for k in range(5)]
        p, m = a + e, a - e
        y[s] = (p + cr) + (br + dr)
        y[16 + s] = (p - cr) + (di - bi)
        f, g = (br - dr) * ROOT, (bi + di) * ROOT
        y[8 + s] = (m - ci) + (f - g)
        y[24 + s] = (m + ci) - (f + g)
    return y


def split(a):
    high = a.astype(BF16)
    return high, (a - high.astype(F32)).astype(BF16)


def matmul(a, matrix):
    return jnp.dot(a, matrix, preferred_element_type=F32)


def product3(high, low, matrix_high, matrix_low):
    return matmul(high, matrix_high) + (matmul(low, matrix_high) + matmul(high, matrix_low))


def kernel(
    queries, keys, values, filters, short_taps, skip, residual, gain, matrices, twist,
    total_f, scale_v, gain_v,
    q_in, k_in, v_in, f_in, r_in, short_weight, skip_gain, mat, tw, tail_kv, halo, ext, mixed, short_q, base,
    send_f, send_m, got_f, got_m, send_y, got_y, a_high, a_low, spec_f, back, sums, own_sum,
    in_sem, halo_send, halo_recv, f_send, f_recv, m_send, m_recv, y_send, y_recv, p_send, p_recv,
):
    parts, rounds = lax.axis_size("seq"), lax.axis_size("ch")
    me, plane = lax.axis_index("seq"), lax.axis_index("ch")
    rows, width = q_in.shape
    own = width // parts
    halves = own // GROUP
    blocks = width // LANES

    barrier = pltpu.get_barrier_semaphore()

    x, y, core = me // 8, lax.rem(me // 2, 4), lax.rem(me, 2)
    peers = [
        lax.rem(x + dx, 4) * 8 + lax.rem(y + dy, 4) * 2 + lax.rem(core + dc, 2)
        for dx, dy, dc in STEPS
    ]
    for peer in peers:
        pl.semaphore_signal(barrier, inc=1, device_id={"seq": peer})

    @pl.loop(1, rounds)
    def _(d):
        pl.semaphore_signal(barrier, inc=1, device_id={"ch": lax.rem(plane + d, rounds)})

    loads = [
        pltpu.make_async_copy(source, target, in_sem.at[i])
        for i, (source, target) in enumerate(
            [
                (filters, f_in), (keys, k_in), (values, v_in), (queries, q_in), (residual, r_in),
                (short_taps, short_weight), (skip, skip_gain), (gain, gain_v),
                (matrices, mat), (twist, tw),
            ]
        )
    ]
    for load in loads:
        load.start()

    def lanes(b):
        return pl.ds(pl.multiple_of(b * LANES, LANES), LANES)

    loads[0].wait()

    @pl.loop(0, blocks)
    def _(b):
        send_f[lanes(b), :] = f_in[:, lanes(b)].T

    for i in (1, 2, 3):
        loads[i].wait()
    last = pl.ds(rows - GROUP, GROUP)
    tail_kv[...] = jnp.concatenate(
        [k_in[last, :].astype(F32)[8:], v_in[last, :].astype(F32)[8:]], axis=0
    ).astype(BF16)

    pl.semaphore_wait(barrier, parts - 1 + rounds - 1)

    after = {"seq": lax.rem(me + 1, parts)}
    tails = [
        pltpu.make_async_remote_copy(
            src_ref=source,
            dst_ref=halo.at[i],
            send_sem=halo_send.at[i],
            recv_sem=halo_recv.at[i],
            device_id=after,
        )
        for i, source in enumerate((tail_kv, q_in.at[pl.ds(rows - GROUP, GROUP), :]))
    ]
    tails[0].start()
    tails[1].start()

    def own_rows(peer, h):
        return pl.ds(pl.multiple_of(h * (width // halves) + peer * GROUP, GROUP), GROUP)

    def exchange_abs(source, target, send_sem, recv_sem):
        pltpu.make_async_copy(source(me), target, recv_sem).start()
        for peer in ABS:
            @pl.when(me != peer)
            def _():
                pltpu.make_async_remote_copy(
                    src_ref=source(peer),
                    dst_ref=target,
                    send_sem=send_sem,
                    recv_sem=recv_sem,
                    device_id={"seq": peer},
                ).start()

    def exchange(source, target, send_sem, recv_sem):
        pltpu.make_async_copy(source(me), target, recv_sem).start()
        for peer in peers:
            pltpu.make_async_remote_copy(
                src_ref=source(peer),
                dst_ref=target,
                send_sem=send_sem,
                recv_sem=recv_sem,
                device_id={"seq": peer},
            ).start()

    for h in range(halves):
        exchange(
            lambda peer: send_f.at[own_rows(peer, h)], got_f.at[h, me], f_send.at[h], f_recv.at[h]
        )

    for i, stream in enumerate((q_in, k_in, v_in)):
        ext[i, pl.ds(8, rows), :] = stream[...].astype(F32)

    def short(i, b, count):
        weights = short_weight[i, :, lanes(b)].astype(F32)
        total = weights[0:1] * ext[i, pl.ds(8, count), lanes(b)]
        for j in range(1, weights.shape[0]):
            total = total + weights[j : j + 1] * ext[i, pl.ds(8 - j, count), lanes(b)]
        return total

    loads[5].wait()
    for i in range(3):
        ext[i, pl.ds(0, 8), :] = jnp.zeros((8, width), F32)

    @pl.loop(0, blocks)
    def _(b):
        product = short(1, b, rows) * short(2, b, rows)
        mixed[:, lanes(b)] = product.astype(BF16)
        send_m[lanes(b), :] = product.astype(BF16).T

    tails[0].wait_recv()
    first = me == 0
    head = jnp.where(first, 0.0, halo[0].astype(F32))
    ext[1, pl.ds(0, 8), :] = head[:8]
    ext[2, pl.ds(0, 8), :] = head[8:]

    for h in range(halves):

        @pl.loop(h * blocks // halves, (h + 1) * blocks // halves)
        def _(b):
            product = short(1, b, GROUP) * short(2, b, GROUP)
            mixed[pl.ds(0, GROUP), lanes(b)] = product.astype(BF16)
            send_m[lanes(b), pl.ds(0, GROUP)] = product.astype(BF16).T

        exchange(
            lambda peer: send_m.at[own_rows(peer, h)], got_m.at[h, me], m_send.at[h], m_recv.at[h]
        )

    loads[8].wait()
    loads[9].wait()

    def twisted(value, i, which):
        cos, sin = tw[which, pl.ds(i, 1), :], tw[which + 1, pl.ds(i, 1), :]
        if value[1] is None:
            return value[0] * cos, value[0] * sin
        return value[0] * cos - value[1] * sin, value[1] * cos + value[0] * sin

    def first_stage(got, h):
        spectrum = forward64([got[h, s].astype(F32) for s in range(PARTS)])
        for k1 in KEPT:
            i = PLACE[k1]
            for half, part in enumerate(twisted(spectrum[k1], i, 0)):
                place = (pl.ds(i * GROUP, GROUP), pl.ds(half * LANES, LANES))
                a_high[place], a_low[place] = split(part)

    @pl.loop(0, halves)
    def _(h):
        pltpu.make_async_copy(got_f.at[h], got_f.at[h], f_recv.at[h]).wait()
        first_stage(got_f, h)
        for c in range(ROWS // CHUNK):
            chunk = pl.ds(c * CHUNK, CHUNK)
            spec_f[h, chunk, :] = product3(a_high[chunk, :], a_low[chunk, :], mat[0], mat[1])

        pltpu.make_async_copy(got_m.at[h], got_m.at[h], m_recv.at[h]).wait()
        first_stage(got_m, h)
        for c in range(ROWS // CHUNK):
            chunk = pl.ds(c * CHUNK, CHUNK)
            signal = product3(a_high[chunk, :], a_low[chunk, :], mat[0], mat[1])
            taps = spec_f[h, chunk, :]
            sr, si = signal[:, :LANES], signal[:, LANES:]
            fr, fi = taps[:, :LANES], taps[:, LANES:]
            both = jnp.concatenate([sr * fr - si * fi, sr * fi + si * fr], axis=1)
            back[chunk, :] = product3(*split(both), mat[2], mat[3])

        def value(k1):
            i = PLACE[k1]
            part = pl.ds(i * GROUP, GROUP)
            return twisted((back[part, pl.ds(0, LANES)], back[part, pl.ds(LANES, LANES)]), i, 2)

        for s, y in enumerate(backward64(value)):
            send_y[h, s] = y.astype(BF16)
        exchange_abs(lambda peer: send_y.at[h, peer], got_y.at[own_rows(me, h)], y_send.at[h], y_recv.at[h])

    tails[1].wait_recv()
    ext[0, pl.ds(0, 8), :] = jnp.where(first, 0.0, halo[1].astype(F32))[8:]
    loads[4].wait()
    loads[6].wait()

    @pl.loop(0, blocks)
    def _(b):
        gate = short(0, b, rows)
        short_q[:, lanes(b)] = gate
        direct = skip_gain[:, lanes(b)] * mixed[:, lanes(b)].astype(F32)
        base[:, lanes(b)] = r_in[:, lanes(b)].astype(F32) + gate * direct

    partial = jnp.zeros((rows, LANES), F32)
    for h in range(halves):
        arrived = got_y.at[pl.ds(h * (width // halves), width // halves)]
        pltpu.make_async_copy(arrived, arrived, y_recv.at[h]).wait()
        for b in range(h * blocks // halves, (h + 1) * blocks // halves):
            at = pl.ds(b * LANES, LANES)
            conv = got_y[at, :].T.astype(F32)
            value = (base[:, at] + short_q[:, at] * conv).astype(BF16).astype(F32)
            total_f[:, at] = value
            partial = partial + value * value

    own_sum[...] = jnp.sum(partial.T, axis=0, keepdims=True)
    pltpu.make_async_copy(own_sum, sums.at[plane], p_recv).start()

    for d in sorted(range(1, rounds), key=lambda d: -min(d, rounds - d)):
        pltpu.make_async_remote_copy(
            src_ref=own_sum,
            dst_ref=sums.at[plane],
            send_sem=p_send,
            recv_sem=p_recv,
            device_id={"ch": lax.rem(plane + d, rounds)},
        ).start()

    for copy in tails:
        copy.wait_send()
    others = pl.ds(0, parts - 1)
    for h in range(halves):
        pass
        pltpu.make_async_copy(got_f.at[h, others], got_f.at[h, others], f_send.at[h]).wait()
        pltpu.make_async_copy(got_m.at[h, others], got_m.at[h, others], m_send.at[h]).wait()
        pltpu.make_async_copy(got_m.at[h, others], got_m.at[h, others], y_send.at[h]).wait()
    if rounds > 1:
        most = sums.at[pl.ds(0, rounds - 1)]
        pltpu.make_async_copy(most, most, p_send).wait()
    loads[7].wait()

    pltpu.make_async_copy(sums, sums, p_recv).wait()
    power = jnp.sum(sums[...], axis=0) / (width * rounds)
    scale_v[...] = lax.rsqrt(power + 1e-05)


def shards(queries, keys, values, filters, short_weight, skip_gain, residual, norm_gain):
    rows, width = queries.shape
    parts, rounds = lax.axis_size("seq"), lax.axis_size("ch")
    taps = short_weight.shape[1]
    own = width // parts
    halves = own // GROUP
    assert parts == PARTS and rows == LANES and own % GROUP == 0
    matrices, twist = tables()
    block = (rows, width)
    whole = pl.BlockSpec(memory_space=pltpu.HBM)
    near = pl.BlockSpec(memory_space=pltpu.VMEM)
    dma = pltpu.SemaphoreType.DMA
    fixed = lambda a: pltpu.with_memory_space_constraint(a, pltpu.HBM)
    total, scale, gain = pl.pallas_call(
        kernel,
        out_shape=(jax.ShapeDtypeStruct(block, F32), jax.ShapeDtypeStruct((1, rows), F32), jax.ShapeDtypeStruct((1, width), F32)),
        in_specs=[whole] * 10,
        out_specs=(near, near, near),
        scratch_shapes=[
            pltpu.VMEM(block, BF16),
            pltpu.VMEM(block, BF16),
            pltpu.VMEM(block, BF16),
            pltpu.VMEM(block, BF16),
            pltpu.VMEM(block, BF16),
            pltpu.VMEM((3, taps, width), BF16),
            pltpu.VMEM((1, width), F32),
            pltpu.VMEM(matrices.shape, BF16),
            pltpu.VMEM(twist.shape, F32),
            pltpu.VMEM((GROUP, width), BF16),
            pltpu.VMEM((2, GROUP, width), BF16),
            pltpu.VMEM((3, rows + 8, width), F32),
            pltpu.VMEM(block, BF16),
            pltpu.VMEM(block, F32),
            pltpu.VMEM(block, F32),
            pltpu.VMEM((width, rows), BF16),
            pltpu.VMEM((width, rows), BF16),
            pltpu.VMEM((halves, parts, GROUP, LANES), BF16),
            pltpu.VMEM((halves, parts, GROUP, LANES), BF16),
            pltpu.VMEM((halves, parts, GROUP, LANES), BF16),
            pltpu.VMEM((width, rows), BF16),
            pltpu.VMEM((ROWS, 2 * LANES), BF16),
            pltpu.VMEM((ROWS, 2 * LANES), BF16),
            pltpu.VMEM((halves, ROWS, 2 * LANES), F32),
            pltpu.VMEM((ROWS, 2 * LANES), F32),
            pltpu.VMEM((rounds, 1, LANES), F32),
            pltpu.VMEM((1, LANES), F32),
            dma((10,)),
            dma((2,)),
            dma((2,)),
            dma((halves,)),
            dma((halves,)),
            dma((halves,)),
            dma((halves,)),
            dma((halves,)),
            dma((halves,)),
            dma,
            dma,
        ],
        compiler_params=pltpu.CompilerParams(
            collective_id=0, has_side_effects=True, vmem_limit_bytes=32 * 1024 * 1024
        ),
        cost_estimate=pl.CostEstimate(flops=2 * 10**9, bytes_accessed=2 * 10**6, transcendentals=0),
    )(
        *[
            fixed(a)
            for a in (
                queries, keys, values, filters, short_weight, skip_gain[None, :], residual, norm_gain[None, :],
                jnp.asarray(matrices), jnp.asarray(twist),
            )
        ]
    )
    stream_out = total.astype(BF16)
    normed = (stream_out.astype(F32) * scale[0][:, None] * gain[0]).astype(BF16)
    return stream_out, normed


def solution(mesh):
    placed = (
        P("seq", "ch"),
        P("seq", "ch"),
        P("seq", "ch"),
        P("seq", "ch"),
        P(None, None, "ch"),
        P("ch"),
        P("seq", "ch"),
        P("ch"),
    )
    return jax.shard_map(
        shards,
        mesh=mesh,
        in_specs=placed,
        out_specs=(P("seq", "ch"), P("seq", "ch")),
        check_vma=False,
    )
```

```python
import functools
import math

import jax
import jax.numpy as jnp
import numpy as np
from jax import lax
from jax.experimental import pallas as pl
from jax.experimental.pallas import tpu as pltpu
from jax.sharding import PartitionSpec as P

F32 = jnp.float32
BF16 = jnp.bfloat16
LANES = 128
GROUP = 16
PARTS = 32
ROOT = math.sqrt(0.5)

KEPT = (
    [0, 8, 16, 24, 32]
    + [1 + 8 * b for b in range(8)]
    + [2 + 8 * b for b in range(8)]
    + [3 + 8 * b for b in range(8)]
    + [4 + 8 * b for b in range(4)]
)
PLACE = {k1: i for i, k1 in enumerate(KEPT)}
ROWS = len(KEPT) * GROUP
CHUNK = 11 * GROUP


STEPS = sorted(
    ((dx, dy, dc) for dx in range(4) for dy in range(4) for dc in range(2) if dx + dy + dc > 0),
    key=lambda step: -(min(step[0], 4 - step[0]) + min(step[1], 4 - step[1])),
)


ABS = sorted(range(32), key=lambda p: (p // 8 + p // 2 % 4, -(p % 2)))


def tables():
    lane = np.arange(LANES)
    angle = 2.0 * np.pi * (np.outer(lane, lane) % LANES) / LANES
    cos, sin = np.cos(angle), np.sin(angle)
    forward = np.block([[cos, -sin], [sin, cos]])
    backward = np.block([[cos, sin], [-sin, cos]])
    parts = []
    for matrix in (forward, backward):
        high = matrix.astype(np.float32).astype(jnp.bfloat16)
        low = (matrix - high.astype(np.float64)).astype(np.float32).astype(jnp.bfloat16)
        parts += [high, low]
    matrices = np.stack(parts)
    turn = 2.0 * np.pi * np.outer(KEPT, lane) / (64 * LANES)
    weight = np.where(np.isin(KEPT, [0, 32]), 1.0, 2.0)[:, None] / (64 * LANES)
    twist = np.stack([np.cos(turn), -np.sin(turn), weight * np.cos(turn), weight * np.sin(turn)])
    return matrices, twist.astype(np.float32)


def plus(a, b):
    if a is None:
        return b
    return a if b is None else a + b


def neg(a):
    return None if a is None else -a


def minus(a, b):
    if b is None:
        return a
    return -b if a is None else a - b


def scaled(a, factor):
    return None if a is None else a * factor


def cplus(a, b):
    return (plus(a[0], b[0]), plus(a[1], b[1]))


def cminus(a, b):
    return (minus(a[0], b[0]), minus(a[1], b[1]))


def quarter(a, sign):
    return (neg(a[1]), a[0]) if sign > 0 else (a[1], neg(a[0]))


def turned(a, angle):
    cos, sin = math.cos(angle), math.sin(angle)
    if angle == 0.0:
        return a
    return (
        minus(scaled(a[0], cos), scaled(a[1], sin)),
        plus(scaled(a[1], cos), scaled(a[0], sin)),
    )


def dft4(z, sign):
    a, b = cplus(z[0], z[2]), cminus(z[0], z[2])
    c, d = cplus(z[1], z[3]), quarter(cminus(z[1], z[3]), sign)
    return [cplus(a, c), cplus(b, d), cminus(a, c), cminus(b, d)]


def dft8(z, sign):
    even, odd = dft4(z[0::2], sign), dft4(z[1::2], sign)
    a, b = odd[1], odd[3]
    if sign > 0:
        first = (scaled(minus(a[0], a[1]), ROOT), scaled(plus(a[0], a[1]), ROOT))
        third = (scaled(plus(b[0], b[1]), -ROOT), scaled(minus(b[0], b[1]), ROOT))
    else:
        first = (scaled(plus(a[0], a[1]), ROOT), scaled(minus(a[1], a[0]), ROOT))
        third = (scaled(minus(b[1], b[0]), ROOT), scaled(plus(b[0], b[1]), -ROOT))
    odd = [odd[0], first, quarter(odd[2], sign), third]
    return [cplus(e, o) for e, o in zip(even, odd)] + [cminus(e, o) for e, o in zip(even, odd)]


def forward64(x):
    column = [[None] * 8 for _ in range(5)]
    for s in range(8):
        x0, x1, x2, x3 = x[s], x[8 + s], x[16 + s], x[24 + s]
        a, b, c, d = x0 + x2, x1 + x3, x0 - x2, (x1 - x3)
        rb, rd = b * ROOT, d * ROOT
        values = [(a + b, None), (x0 + rd, -x2 - rb), (c, -d), (x0 - rd, x2 - rb), (a - b, None)]
        for k in range(5):
            column[k][s] = turned(values[k], -2.0 * math.pi * s * k / 64)
    out = {}
    for k in range(5):
        result = dft8(column[k], -1)
        for b in range((5, 8, 8, 8, 4)[k]):
            out[k + 8 * b] = result[b]
    return out


def backward64(get):
    v = []
    for k in range(5):
        count = (5, 8, 8, 8, 4)[k]
        z = [get(k + 8 * b) if b < count else (None, None) for b in range(8)]
        if k == 0:
            z[0], z[4] = (z[0][0], None), (z[4][0], None)
        u = dft8(z, 1)
        v.append([turned(u[s], 2.0 * math.pi * s * k / 64) for s in range(8)])
    y = [None] * 32
    for s in range(8):
        (a, _), (br, bi), (cr, ci), (dr, di), (e, _) = [v[k][s] for k in range(5)]
        p, m = a + e, a - e
        y[s] = (p + cr) + (br + dr)
        y[16 + s] = (p - cr) + (di - bi)
        f, g = (br - dr) * ROOT, (bi + di) * ROOT
        y[8 + s] = (m - ci) + (f - g)
        y[24 + s] = (m + ci) - (f + g)
    return y


def split(a):
    high = a.astype(BF16)
    return high, (a - high.astype(F32)).astype(BF16)


def matmul(a, matrix):
    return jnp.dot(a, matrix, preferred_element_type=F32)


def product3(high, low, matrix_high, matrix_low):
    return matmul(high, matrix_high) + (matmul(low, matrix_high) + matmul(high, matrix_low))


def kernel(
    queries, keys, values, filters, short_taps, skip, residual, gain, matrices, twist,
    total_f, scale_v, gain_v,
    q_in, k_in, v_in, f_in, r_in, short_weight, skip_gain, mat, tw, tail_kv, halo, ext, mixed, short_q, base,
    send_f, send_m, got_f, got_m, send_y, got_y, a_high, a_low, spec_f, back, sums, own_sum,
    in_sem, halo_send, halo_recv, f_send, f_recv, m_send, m_recv, y_send, y_recv, p_send, p_recv,
):
    parts, rounds = lax.axis_size("seq"), lax.axis_size("ch")
    me, plane = lax.axis_index("seq"), lax.axis_index("ch")
    rows, width = q_in.shape
    own = width // parts
    halves = own // GROUP
    blocks = width // LANES

    barrier = pltpu.get_barrier_semaphore()

    x, y, core = me // 8, lax.rem(me // 2, 4), lax.rem(me, 2)
    peers = [
        lax.rem(x + dx, 4) * 8 + lax.rem(y + dy, 4) * 2 + lax.rem(core + dc, 2)
        for dx, dy, dc in STEPS
    ]
    for peer in peers:
        pl.semaphore_signal(barrier, inc=1, device_id={"seq": peer})

    @pl.loop(1, rounds)
    def _(d):
        pl.semaphore_signal(barrier, inc=1, device_id={"ch": lax.rem(plane + d, rounds)})

    loads = [
        pltpu.make_async_copy(source, target, in_sem.at[i])
        for i, (source, target) in enumerate(
            [
                (keys, k_in), (values, v_in), (queries, q_in), (filters, f_in), (residual, r_in),
                (short_taps, short_weight), (skip, skip_gain), (gain, gain_v),
                (matrices, mat), (twist, tw),
            ]
        )
    ]
    for load in loads:
        load.start()

    def lanes(b):
        return pl.ds(pl.multiple_of(b * LANES, LANES), LANES)

    for i in (0, 1, 2):
        loads[i].wait()
    last = pl.ds(rows - GROUP, GROUP)
    tail_kv[...] = jnp.concatenate(
        [k_in[last, :].astype(F32)[8:], v_in[last, :].astype(F32)[8:]], axis=0
    ).astype(BF16)

    pl.semaphore_wait(barrier, parts - 1 + rounds - 1)

    after = {"seq": lax.rem(me + 1, parts)}
    tails = [
        pltpu.make_async_remote_copy(
            src_ref=source,
            dst_ref=halo.at[i],
            send_sem=halo_send.at[i],
            recv_sem=halo_recv.at[i],
            device_id=after,
        )
        for i, source in enumerate((tail_kv, q_in.at[pl.ds(rows - GROUP, GROUP), :]))
    ]
    tails[0].start()
    tails[1].start()

    loads[3].wait()

    @pl.loop(0, blocks)
    def _(b):
        send_f[lanes(b), :] = f_in[:, lanes(b)].T

    def own_rows(peer, h):
        return pl.ds(pl.multiple_of(h * (width // halves) + peer * GROUP, GROUP), GROUP)

    def exchange_abs(source, target, send_sem, recv_sem):
        pltpu.make_async_copy(source(me), target, recv_sem).start()
        for peer in ABS:
            @pl.when(me != peer)
            def _():
                pltpu.make_async_remote_copy(
                    src_ref=source(peer),
                    dst_ref=target,
                    send_sem=send_sem,
                    recv_sem=recv_sem,
                    device_id={"seq": peer},
                ).start()

    def exchange(source, target, send_sem, recv_sem):
        pltpu.make_async_copy(source(me), target, recv_sem).start()
        for peer in peers:
            pltpu.make_async_remote_copy(
                src_ref=source(peer),
                dst_ref=target,
                send_sem=send_sem,
                recv_sem=recv_sem,
                device_id={"seq": peer},
            ).start()

    for h in range(halves):
        exchange(
            lambda peer: send_f.at[own_rows(peer, h)], got_f.at[h, me], f_send.at[h], f_recv.at[h]
        )

    for i, stream in enumerate((q_in, k_in, v_in)):
        ext[i, pl.ds(8, rows), :] = stream[...].astype(F32)

    def short(i, b, count):
        weights = short_weight[i, :, lanes(b)].astype(F32)
        total = weights[0:1] * ext[i, pl.ds(8, count), lanes(b)]
        for j in range(1, weights.shape[0]):
            total = total + weights[j : j + 1] * ext[i, pl.ds(8 - j, count), lanes(b)]
        return total

    loads[5].wait()
    for i in range(3):
        ext[i, pl.ds(0, 8), :] = jnp.zeros((8, width), F32)

    @pl.loop(0, blocks)
    def _(b):
        product = short(1, b, rows) * short(2, b, rows)
        mixed[:, lanes(b)] = product.astype(BF16)
        send_m[lanes(b), :] = product.astype(BF16).T

    tails[0].wait_recv()
    first = me == 0
    head = jnp.where(first, 0.0, halo[0].astype(F32))
    ext[1, pl.ds(0, 8), :] = head[:8]
    ext[2, pl.ds(0, 8), :] = head[8:]

    for h in range(halves):

        @pl.loop(h * blocks // halves, (h + 1) * blocks // halves)
        def _(b):
            product = short(1, b, GROUP) * short(2, b, GROUP)
            mixed[pl.ds(0, GROUP), lanes(b)] = product.astype(BF16)
            send_m[lanes(b), pl.ds(0, GROUP)] = product.astype(BF16).T

        exchange(
            lambda peer: send_m.at[own_rows(peer, h)], got_m.at[h, me], m_send.at[h], m_recv.at[h]
        )

    loads[8].wait()
    loads[9].wait()

    def twisted(value, i, which):
        cos, sin = tw[which, pl.ds(i, 1), :], tw[which + 1, pl.ds(i, 1), :]
        if value[1] is None:
            return value[0] * cos, value[0] * sin
        return value[0] * cos - value[1] * sin, value[1] * cos + value[0] * sin

    def first_stage(got, h):
        spectrum = forward64([got[h, s].astype(F32) for s in range(PARTS)])
        for k1 in KEPT:
            i = PLACE[k1]
            for half, part in enumerate(twisted(spectrum[k1], i, 0)):
                place = (pl.ds(i * GROUP, GROUP), pl.ds(half * LANES, LANES))
                a_high[place], a_low[place] = split(part)

    @pl.loop(0, halves)
    def _(h):
        pltpu.make_async_copy(got_f.at[h], got_f.at[h], f_recv.at[h]).wait()
        first_stage(got_f, h)
        for c in range(ROWS // CHUNK):
            chunk = pl.ds(c * CHUNK, CHUNK)
            spec_f[h, chunk, :] = product3(a_high[chunk, :], a_low[chunk, :], mat[0], mat[1])

    @pl.loop(0, halves)
    def _(h):
        pass
        pltpu.make_async_copy(got_m.at[h], got_m.at[h], m_recv.at[h]).wait()
        first_stage(got_m, h)
        for c in range(ROWS // CHUNK):
            chunk = pl.ds(c * CHUNK, CHUNK)
            signal = product3(a_high[chunk, :], a_low[chunk, :], mat[0], mat[1])
            taps = spec_f[h, chunk, :]
            sr, si = signal[:, :LANES], signal[:, LANES:]
            fr, fi = taps[:, :LANES], taps[:, LANES:]
            both = jnp.concatenate([sr * fr - si * fi, sr * fi + si * fr], axis=1)
            back[chunk, :] = product3(*split(both), mat[2], mat[3])

        def value(k1):
            i = PLACE[k1]
            part = pl.ds(i * GROUP, GROUP)
            return twisted((back[part, pl.ds(0, LANES)], back[part, pl.ds(LANES, LANES)]), i, 2)

        for s, y in enumerate(backward64(value)):
            send_y[h, s] = y.astype(BF16)
        exchange_abs(lambda peer: send_y.at[h, peer], got_y.at[own_rows(me, h)], y_send.at[h], y_recv.at[h])

    tails[1].wait_recv()
    ext[0, pl.ds(0, 8), :] = jnp.where(first, 0.0, halo[1].astype(F32))[8:]
    loads[4].wait()
    loads[6].wait()

    @pl.loop(0, blocks)
    def _(b):
        gate = short(0, b, rows)
        short_q[:, lanes(b)] = gate
        direct = skip_gain[:, lanes(b)] * mixed[:, lanes(b)].astype(F32)
        base[:, lanes(b)] = r_in[:, lanes(b)].astype(F32) + gate * direct

    partial = jnp.zeros((rows, LANES), F32)
    for h in range(halves):
        arrived = got_y.at[pl.ds(h * (width // halves), width // halves)]
        pltpu.make_async_copy(arrived, arrived, y_recv.at[h]).wait()
        for b in range(h * blocks // halves, (h + 1) * blocks // halves):
            at = pl.ds(b * LANES, LANES)
            conv = got_y[at, :].T.astype(F32)
            value = (base[:, at] + short_q[:, at] * conv).astype(BF16).astype(F32)
            total_f[:, at] = value
            partial = partial + value * value

    own_sum[...] = jnp.sum(partial.T, axis=0, keepdims=True)
    pltpu.make_async_copy(own_sum, sums.at[plane], p_recv).start()

    for d in sorted(range(1, rounds), key=lambda d: -min(d, rounds - d)):
        pltpu.make_async_remote_copy(
            src_ref=own_sum,
            dst_ref=sums.at[plane],
            send_sem=p_send,
            recv_sem=p_recv,
            device_id={"ch": lax.rem(plane + d, rounds)},
        ).start()

    for copy in tails:
        copy.wait_send()
    others = pl.ds(0, parts - 1)
    for h in range(halves):
        pass
        pltpu.make_async_copy(got_f.at[h, others], got_f.at[h, others], f_send.at[h]).wait()
        pltpu.make_async_copy(got_m.at[h, others], got_m.at[h, others], m_send.at[h]).wait()
        pltpu.make_async_copy(got_m.at[h, others], got_m.at[h, others], y_send.at[h]).wait()
    if rounds > 1:
        most = sums.at[pl.ds(0, rounds - 1)]
        pltpu.make_async_copy(most, most, p_send).wait()
    loads[7].wait()

    pltpu.make_async_copy(sums, sums, p_recv).wait()
    power = jnp.sum(sums[...], axis=0) / (width * rounds)
    scale_v[...] = lax.rsqrt(power + 1e-05)


def shards(queries, keys, values, filters, short_weight, skip_gain, residual, norm_gain):
    rows, width = queries.shape
    parts, rounds = lax.axis_size("seq"), lax.axis_size("ch")
    taps = short_weight.shape[1]
    own = width // parts
    halves = own // GROUP
    assert parts == PARTS and rows == LANES and own % GROUP == 0
    matrices, twist = tables()
    block = (rows, width)
    whole = pl.BlockSpec(memory_space=pltpu.HBM)
    near = pl.BlockSpec(memory_space=pltpu.VMEM)
    dma = pltpu.SemaphoreType.DMA
    fixed = lambda a: pltpu.with_memory_space_constraint(a, pltpu.HBM)
    total, scale, gain = pl.pallas_call(
        kernel,
        out_shape=(jax.ShapeDtypeStruct(block, F32), jax.ShapeDtypeStruct((1, rows), F32), jax.ShapeDtypeStruct((1, width), F32)),
        in_specs=[whole] * 10,
        out_specs=(near, near, near),
        scratch_shapes=[
            pltpu.VMEM(block, BF16),
            pltpu.VMEM(block, BF16),
            pltpu.VMEM(block, BF16),
            pltpu.VMEM(block, BF16),
            pltpu.VMEM(block, BF16),
            pltpu.VMEM((3, taps, width), BF16),
            pltpu.VMEM((1, width), F32),
            pltpu.VMEM(matrices.shape, BF16),
            pltpu.VMEM(twist.shape, F32),
            pltpu.VMEM((GROUP, width), BF16),
            pltpu.VMEM((2, GROUP, width), BF16),
            pltpu.VMEM((3, rows + 8, width), F32),
            pltpu.VMEM(block, BF16),
            pltpu.VMEM(block, F32),
            pltpu.VMEM(block, F32),
            pltpu.VMEM((width, rows), BF16),
            pltpu.VMEM((width, rows), BF16),
            pltpu.VMEM((halves, parts, GROUP, LANES), BF16),
            pltpu.VMEM((halves, parts, GROUP, LANES), BF16),
            pltpu.VMEM((halves, parts, GROUP, LANES), BF16),
            pltpu.VMEM((width, rows), BF16),
            pltpu.VMEM((ROWS, 2 * LANES), BF16),
            pltpu.VMEM((ROWS, 2 * LANES), BF16),
            pltpu.VMEM((halves, ROWS, 2 * LANES), F32),
            pltpu.VMEM((ROWS, 2 * LANES), F32),
            pltpu.VMEM((rounds, 1, LANES), F32),
            pltpu.VMEM((1, LANES), F32),
            dma((10,)),
            dma((2,)),
            dma((2,)),
            dma((halves,)),
            dma((halves,)),
            dma((halves,)),
            dma((halves,)),
            dma((halves,)),
            dma((halves,)),
            dma,
            dma,
        ],
        compiler_params=pltpu.CompilerParams(
            collective_id=0, has_side_effects=True, vmem_limit_bytes=32 * 1024 * 1024
        ),
        cost_estimate=pl.CostEstimate(flops=2 * 10**9, bytes_accessed=2 * 10**6, transcendentals=0),
    )(
        *[
            fixed(a)
            for a in (
                queries, keys, values, filters, short_weight, skip_gain[None, :], residual, norm_gain[None, :],
                jnp.asarray(matrices), jnp.asarray(twist),
            )
        ]
    )
    stream_out = total.astype(BF16)
    normed = (stream_out.astype(F32) * scale[0][:, None] * gain[0]).astype(BF16)
    return stream_out, normed


def solution(mesh):
    placed = (
        P("seq", "ch"),
        P("seq", "ch"),
        P("seq", "ch"),
        P("seq", "ch"),
        P(None, None, "ch"),
        P("ch"),
        P("seq", "ch"),
        P("ch"),
    )
    return jax.shard_map(
        shards,
        mesh=mesh,
        in_specs=placed,
        out_specs=(P("seq", "ch"), P("seq", "ch")),
        check_vma=False,
    )
```

```python
import functools
import math

import jax
import jax.numpy as jnp
import numpy as np
from jax import lax
from jax.experimental import pallas as pl
from jax.experimental.pallas import tpu as pltpu
from jax.sharding import PartitionSpec as P

F32 = jnp.float32
BF16 = jnp.bfloat16
LANES = 128
GROUP = 16
PARTS = 32
ROOT = math.sqrt(0.5)

KEPT = (
    [0, 8, 16, 24, 32]
    + [1 + 8 * b for b in range(8)]
    + [2 + 8 * b for b in range(8)]
    + [3 + 8 * b for b in range(8)]
    + [4 + 8 * b for b in range(4)]
)
PLACE = {k1: i for i, k1 in enumerate(KEPT)}
ROWS = len(KEPT) * GROUP
CHUNK = 33 * GROUP


STEPS = sorted(
    ((dx, dy, dc) for dx in range(4) for dy in range(4) for dc in range(2) if dx + dy + dc > 0),
    key=lambda step: -(min(step[0], 4 - step[0]) + min(step[1], 4 - step[1])),
)


ABS = sorted(range(32), key=lambda p: (p // 8 + p // 2 % 4, -(p % 2)))


def tables():
    lane = np.arange(LANES)
    angle = 2.0 * np.pi * (np.outer(lane, lane) % LANES) / LANES
    cos, sin = np.cos(angle), np.sin(angle)
    forward = np.block([[cos, -sin], [sin, cos]])
    backward = np.block([[cos, sin], [-sin, cos]])
    parts = []
    for matrix in (forward, backward):
        high = matrix.astype(np.float32).astype(jnp.bfloat16)
        low = (matrix - high.astype(np.float64)).astype(np.float32).astype(jnp.bfloat16)
        parts += [high, low]
    matrices = np.stack(parts)
    turn = 2.0 * np.pi * np.outer(KEPT, lane) / (64 * LANES)
    weight = np.where(np.isin(KEPT, [0, 32]), 1.0, 2.0)[:, None] / (64 * LANES)
    twist = np.stack([np.cos(turn), -np.sin(turn), weight * np.cos(turn), weight * np.sin(turn)])
    return matrices, twist.astype(np.float32)


def plus(a, b):
    if a is None:
        return b
    return a if b is None else a + b


def neg(a):
    return None if a is None else -a


def minus(a, b):
    if b is None:
        return a
    return -b if a is None else a - b


def scaled(a, factor):
    return None if a is None else a * factor


def cplus(a, b):
    return (plus(a[0], b[0]), plus(a[1], b[1]))


def cminus(a, b):
    return (minus(a[0], b[0]), minus(a[1], b[1]))


def quarter(a, sign):
    return (neg(a[1]), a[0]) if sign > 0 else (a[1], neg(a[0]))


def turned(a, angle):
    cos, sin = math.cos(angle), math.sin(angle)
    if angle == 0.0:
        return a
    return (
        minus(scaled(a[0], cos), scaled(a[1], sin)),
        plus(scaled(a[1], cos), scaled(a[0], sin)),
    )


def dft4(z, sign):
    a, b = cplus(z[0], z[2]), cminus(z[0], z[2])
    c, d = cplus(z[1], z[3]), quarter(cminus(z[1], z[3]), sign)
    return [cplus(a, c), cplus(b, d), cminus(a, c), cminus(b, d)]


def dft8(z, sign):
    even, odd = dft4(z[0::2], sign), dft4(z[1::2], sign)
    a, b = odd[1], odd[3]
    if sign > 0:
        first = (scaled(minus(a[0], a[1]), ROOT), scaled(plus(a[0], a[1]), ROOT))
        third = (scaled(plus(b[0], b[1]), -ROOT), scaled(minus(b[0], b[1]), ROOT))
    else:
        first = (scaled(plus(a[0], a[1]), ROOT), scaled(minus(a[1], a[0]), ROOT))
        third = (scaled(minus(b[1], b[0]), ROOT), scaled(plus(b[0], b[1]), -ROOT))
    odd = [odd[0], first, quarter(odd[2], sign), third]
    return [cplus(e, o) for e, o in zip(even, odd)] + [cminus(e, o) for e, o in zip(even, odd)]


def forward64(x):
    column = [[None] * 8 for _ in range(5)]
    for s in range(8):
        x0, x1, x2, x3 = x[s], x[8 + s], x[16 + s], x[24 + s]
        a, b, c, d = x0 + x2, x1 + x3, x0 - x2, (x1 - x3)
        rb, rd = b * ROOT, d * ROOT
        values = [(a + b, None), (x0 + rd, -x2 - rb), (c, -d), (x0 - rd, x2 - rb), (a - b, None)]
        for k in range(5):
            column[k][s] = turned(values[k], -2.0 * math.pi * s * k / 64)
    out = {}
    for k in range(5):
        result = dft8(column[k], -1)
        for b in range((5, 8, 8, 8, 4)[k]):
            out[k + 8 * b] = result[b]
    return out


def backward64(get):
    v = []
    for k in range(5):
        count = (5, 8, 8, 8, 4)[k]
        z = [get(k + 8 * b) if b < count else (None, None) for b in range(8)]
        if k == 0:
            z[0], z[4] = (z[0][0], None), (z[4][0], None)
        u = dft8(z, 1)
        v.append([turned(u[s], 2.0 * math.pi * s * k / 64) for s in range(8)])
    y = [None] * 32
    for s in range(8):
        (a, _), (br, bi), (cr, ci), (dr, di), (e, _) = [v[k][s] for k in range(5)]
        p, m = a + e, a - e
        y[s] = (p + cr) + (br + dr)
        y[16 + s] = (p - cr) + (di - bi)
        f, g = (br - dr) * ROOT, (bi + di) * ROOT
        y[8 + s] = (m - ci) + (f - g)
        y[24 + s] = (m + ci) - (f + g)
    return y


def split(a):
    high = a.astype(BF16)
    return high, (a - high.astype(F32)).astype(BF16)


def matmul(a, matrix):
    return jnp.dot(a, matrix, preferred_element_type=F32)


def product3(high, low, matrix_high, matrix_low):
    return matmul(high, matrix_high) + (matmul(low, matrix_high) + matmul(high, matrix_low))


def kernel(
    queries, keys, values, filters, short_taps, skip, residual, gain, matrices, twist,
    total_f, scale_v, gain_v,
    q_in, k_in, v_in, f_in, r_in, short_weight, skip_gain, mat, tw, tail_kv, halo, ext, mixed, short_q, base,
    send_f, send_m, got_f, got_m, send_y, got_y, a_high, a_low, spec_f, back, sums, own_sum,
    in_sem, halo_send, halo_recv, f_send, f_recv, m_send, m_recv, y_send, y_recv, p_send, p_recv,
):
    parts, rounds = lax.axis_size("seq"), lax.axis_size("ch")
    me, plane = lax.axis_index("seq"), lax.axis_index("ch")
    rows, width = q_in.shape
    own = width // parts
    halves = own // GROUP
    blocks = width // LANES

    barrier = pltpu.get_barrier_semaphore()

    x, y, core = me // 8, lax.rem(me // 2, 4), lax.rem(me, 2)
    peers = [
        lax.rem(x + dx, 4) * 8 + lax.rem(y + dy, 4) * 2 + lax.rem(core + dc, 2)
        for dx, dy, dc in STEPS
    ]
    for peer in peers:
        pl.semaphore_signal(barrier, inc=1, device_id={"seq": peer})

    @pl.loop(1, rounds)
    def _(d):
        pl.semaphore_signal(barrier, inc=1, device_id={"ch": lax.rem(plane + d, rounds)})

    loads = [
        pltpu.make_async_copy(source, target, in_sem.at[i])
        for i, (source, target) in enumerate(
            [
                (filters, f_in), (keys, k_in), (values, v_in), (queries, q_in), (residual, r_in),
                (short_taps, short_weight), (skip, skip_gain), (gain, gain_v),
                (matrices, mat), (twist, tw),
            ]
        )
    ]
    for load in loads:
        load.start()

    def lanes(b):
        return pl.ds(pl.multiple_of(b * LANES, LANES), LANES)

    loads[0].wait()

    @pl.loop(0, blocks)
    def _(b):
        send_f[lanes(b), :] = f_in[:, lanes(b)].T

    for i in (1, 2, 3):
        loads[i].wait()
    last = pl.ds(rows - GROUP, GROUP)
    tail_kv[...] = jnp.concatenate(
        [k_in[last, :].astype(F32)[8:], v_in[last, :].astype(F32)[8:]], axis=0
    ).astype(BF16)

    pl.semaphore_wait(barrier, parts - 1 + rounds - 1)

    after = {"seq": lax.rem(me + 1, parts)}
    tails = [
        pltpu.make_async_remote_copy(
            src_ref=source,
            dst_ref=halo.at[i],
            send_sem=halo_send.at[i],
            recv_sem=halo_recv.at[i],
            device_id=after,
        )
        for i, source in enumerate((tail_kv, q_in.at[pl.ds(rows - GROUP, GROUP), :]))
    ]
    tails[0].start()
    tails[1].start()

    def own_rows(peer, h):
        return pl.ds(pl.multiple_of(h * (width // halves) + peer * GROUP, GROUP), GROUP)

    def exchange_abs(source, target, send_sem, recv_sem):
        pltpu.make_async_copy(source(me), target, recv_sem).start()
        for peer in ABS:
            @pl.when(me != peer)
            def _():
                pltpu.make_async_remote_copy(
                    src_ref=source(peer),
                    dst_ref=target,
                    send_sem=send_sem,
                    recv_sem=recv_sem,
                    device_id={"seq": peer},
                ).start()

    def exchange(source, target, send_sem, recv_sem):
        pltpu.make_async_copy(source(me), target, recv_sem).start()
        for peer in peers:
            pltpu.make_async_remote_copy(
                src_ref=source(peer),
                dst_ref=target,
                send_sem=send_sem,
                recv_sem=recv_sem,
                device_id={"seq": peer},
            ).start()

    for h in range(halves):
        exchange(
            lambda peer: send_f.at[own_rows(peer, h)], got_f.at[h, me], f_send.at[h], f_recv.at[h]
        )

    for i, stream in enumerate((q_in, k_in, v_in)):
        ext[i, pl.ds(8, rows), :] = stream[...].astype(F32)

    def short(i, b, count):
        weights = short_weight[i, :, lanes(b)].astype(F32)
        total = weights[0:1] * ext[i, pl.ds(8, count), lanes(b)]
        for j in range(1, weights.shape[0]):
            total = total + weights[j : j + 1] * ext[i, pl.ds(8 - j, count), lanes(b)]
        return total

    loads[5].wait()
    for i in range(3):
        ext[i, pl.ds(0, 8), :] = jnp.zeros((8, width), F32)

    @pl.loop(0, blocks)
    def _(b):
        product = short(1, b, rows) * short(2, b, rows)
        mixed[:, lanes(b)] = product.astype(BF16)
        send_m[lanes(b), :] = product.astype(BF16).T

    tails[0].wait_recv()
    first = me == 0
    head = jnp.where(first, 0.0, halo[0].astype(F32))
    ext[1, pl.ds(0, 8), :] = head[:8]
    ext[2, pl.ds(0, 8), :] = head[8:]

    for h in range(halves):

        @pl.loop(h * blocks // halves, (h + 1) * blocks // halves)
        def _(b):
            product = short(1, b, GROUP) * short(2, b, GROUP)
            mixed[pl.ds(0, GROUP), lanes(b)] = product.astype(BF16)
            send_m[lanes(b), pl.ds(0, GROUP)] = product.astype(BF16).T

        exchange(
            lambda peer: send_m.at[own_rows(peer, h)], got_m.at[h, me], m_send.at[h], m_recv.at[h]
        )

    loads[8].wait()
    loads[9].wait()

    def twisted(value, i, which):
        cos, sin = tw[which, pl.ds(i, 1), :], tw[which + 1, pl.ds(i, 1), :]
        if value[1] is None:
            return value[0] * cos, value[0] * sin
        return value[0] * cos - value[1] * sin, value[1] * cos + value[0] * sin

    def first_stage(got, h):
        spectrum = forward64([got[h, s].astype(F32) for s in range(PARTS)])
        for k1 in KEPT:
            i = PLACE[k1]
            for half, part in enumerate(twisted(spectrum[k1], i, 0)):
                place = (pl.ds(i * GROUP, GROUP), pl.ds(half * LANES, LANES))
                a_high[place], a_low[place] = split(part)

    @pl.loop(0, halves)
    def _(h):
        pltpu.make_async_copy(got_f.at[h], got_f.at[h], f_recv.at[h]).wait()
        first_stage(got_f, h)
        for c in range(ROWS // CHUNK):
            chunk = pl.ds(c * CHUNK, CHUNK)
            spec_f[h, chunk, :] = product3(a_high[chunk, :], a_low[chunk, :], mat[0], mat[1])

    @pl.loop(0, halves)
    def _(h):
        pass
        pltpu.make_async_copy(got_m.at[h], got_m.at[h], m_recv.at[h]).wait()
        first_stage(got_m, h)
        for c in range(ROWS // CHUNK):
            chunk = pl.ds(c * CHUNK, CHUNK)
            signal = product3(a_high[chunk, :], a_low[chunk, :], mat[0], mat[1])
            taps = spec_f[h, chunk, :]
            sr, si = signal[:, :LANES], signal[:, LANES:]
            fr, fi = taps[:, :LANES], taps[:, LANES:]
            both = jnp.concatenate([sr * fr - si * fi, sr * fi + si * fr], axis=1)
            back[chunk, :] = product3(*split(both), mat[2], mat[3])

        def value(k1):
            i = PLACE[k1]
            part = pl.ds(i * GROUP, GROUP)
            return twisted((back[part, pl.ds(0, LANES)], back[part, pl.ds(LANES, LANES)]), i, 2)

        for s, y in enumerate(backward64(value)):
            send_y[h, s] = y.astype(BF16)
        exchange_abs(lambda peer: send_y.at[h, peer], got_y.at[own_rows(me, h)], y_send.at[h], y_recv.at[h])

    tails[1].wait_recv()
    ext[0, pl.ds(0, 8), :] = jnp.where(first, 0.0, halo[1].astype(F32))[8:]
    loads[4].wait()
    loads[6].wait()

    @pl.loop(0, blocks)
    def _(b):
        gate = short(0, b, rows)
        short_q[:, lanes(b)] = gate
        direct = skip_gain[:, lanes(b)] * mixed[:, lanes(b)].astype(F32)
        base[:, lanes(b)] = r_in[:, lanes(b)].astype(F32) + gate * direct

    partial = jnp.zeros((rows, LANES), F32)
    for h in range(halves):
        arrived = got_y.at[pl.ds(h * (width // halves), width // halves)]
        pltpu.make_async_copy(arrived, arrived, y_recv.at[h]).wait()
        for b in range(h * blocks // halves, (h + 1) * blocks // halves):
            at = pl.ds(b * LANES, LANES)
            conv = got_y[at, :].T.astype(F32)
            value = (base[:, at] + short_q[:, at] * conv).astype(BF16).astype(F32)
            total_f[:, at] = value
            partial = partial + value * value

    own_sum[...] = jnp.sum(partial.T, axis=0, keepdims=True)
    pltpu.make_async_copy(own_sum, sums.at[plane], p_recv).start()

    for d in sorted(range(1, rounds), key=lambda d: -min(d, rounds - d)):
        pltpu.make_async_remote_copy(
            src_ref=own_sum,
            dst_ref=sums.at[plane],
            send_sem=p_send,
            recv_sem=p_recv,
            device_id={"ch": lax.rem(plane + d, rounds)},
        ).start()

    for copy in tails:
        copy.wait_send()
    others = pl.ds(0, parts - 1)
    for h in range(halves):
        pass
        pltpu.make_async_copy(got_f.at[h, others], got_f.at[h, others], f_send.at[h]).wait()
        pltpu.make_async_copy(got_m.at[h, others], got_m.at[h, others], m_send.at[h]).wait()
        pltpu.make_async_copy(got_m.at[h, others], got_m.at[h, others], y_send.at[h]).wait()
    if rounds > 1:
        most = sums.at[pl.ds(0, rounds - 1)]
        pltpu.make_async_copy(most, most, p_send).wait()
    loads[7].wait()

    pltpu.make_async_copy(sums, sums, p_recv).wait()
    power = jnp.sum(sums[...], axis=0) / (width * rounds)
    scale_v[...] = lax.rsqrt(power + 1e-05)


def shards(queries, keys, values, filters, short_weight, skip_gain, residual, norm_gain):
    rows, width = queries.shape
    parts, rounds = lax.axis_size("seq"), lax.axis_size("ch")
    taps = short_weight.shape[1]
    own = width // parts
    halves = own // GROUP
    assert parts == PARTS and rows == LANES and own % GROUP == 0
    matrices, twist = tables()
    block = (rows, width)
    whole = pl.BlockSpec(memory_space=pltpu.HBM)
    near = pl.BlockSpec(memory_space=pltpu.VMEM)
    dma = pltpu.SemaphoreType.DMA
    fixed = lambda a: pltpu.with_memory_space_constraint(a, pltpu.HBM)
    total, scale, gain = pl.pallas_call(
        kernel,
        out_shape=(jax.ShapeDtypeStruct(block, F32), jax.ShapeDtypeStruct((1, rows), F32), jax.ShapeDtypeStruct((1, width), F32)),
        in_specs=[whole] * 10,
        out_specs=(near, near, near),
        scratch_shapes=[
            pltpu.VMEM(block, BF16),
            pltpu.VMEM(block, BF16),
            pltpu.VMEM(block, BF16),
            pltpu.VMEM(block, BF16),
            pltpu.VMEM(block, BF16),
            pltpu.VMEM((3, taps, width), BF16),
            pltpu.VMEM((1, width), F32),
            pltpu.VMEM(matrices.shape, BF16),
            pltpu.VMEM(twist.shape, F32),
            pltpu.VMEM((GROUP, width), BF16),
            pltpu.VMEM((2, GROUP, width), BF16),
            pltpu.VMEM((3, rows + 8, width), F32),
            pltpu.VMEM(block, BF16),
            pltpu.VMEM(block, F32),
            pltpu.VMEM(block, F32),
            pltpu.VMEM((width, rows), BF16),
            pltpu.VMEM((width, rows), BF16),
            pltpu.VMEM((halves, parts, GROUP, LANES), BF16),
            pltpu.VMEM((halves, parts, GROUP, LANES), BF16),
            pltpu.VMEM((halves, parts, GROUP, LANES), BF16),
            pltpu.VMEM((width, rows), BF16),
            pltpu.VMEM((ROWS, 2 * LANES), BF16),
            pltpu.VMEM((ROWS, 2 * LANES), BF16),
            pltpu.VMEM((halves, ROWS, 2 * LANES), F32),
            pltpu.VMEM((ROWS, 2 * LANES), F32),
            pltpu.VMEM((rounds, 1, LANES), F32),
            pltpu.VMEM((1, LANES), F32),
            dma((10,)),
            dma((2,)),
            dma((2,)),
            dma((halves,)),
            dma((halves,)),
            dma((halves,)),
            dma((halves,)),
            dma((halves,)),
            dma((halves,)),
            dma,
            dma,
        ],
        compiler_params=pltpu.CompilerParams(
            collective_id=0, has_side_effects=True, vmem_limit_bytes=32 * 1024 * 1024
        ),
        cost_estimate=pl.CostEstimate(flops=2 * 10**9, bytes_accessed=2 * 10**6, transcendentals=0),
    )(
        *[
            fixed(a)
            for a in (
                queries, keys, values, filters, short_weight, skip_gain[None, :], residual, norm_gain[None, :],
                jnp.asarray(matrices), jnp.asarray(twist),
            )
        ]
    )
    stream_out = total.astype(BF16)
    normed = (stream_out.astype(F32) * scale[0][:, None] * gain[0]).astype(BF16)
    return stream_out, normed


def solution(mesh):
    placed = (
        P("seq", "ch"),
        P("seq", "ch"),
        P("seq", "ch"),
        P("seq", "ch"),
        P(None, None, "ch"),
        P("ch"),
        P("seq", "ch"),
        P("ch"),
    )
    return jax.shard_map(
        shards,
        mesh=mesh,
        in_specs=placed,
        out_specs=(P("seq", "ch"), P("seq", "ch")),
        check_vma=False,
    )
```
